256 devices in a mesh: row: 16 (over x_lo, y, core), col: 16 (over x_hi, z).
Axes of the slice: x: 4 (x_hi: 2, x_lo: 2; x = x_hi * 2 + x_lo), y: 4, z: 8, core: 2. Of those that a mesh axis runs over, the one named last changes fastest.
Arguments:
- tokens: bfloat16 [4096, 12288], P('row', 'col'), may hold values from -500 to 500
- ln_gain: bfloat16 [12288], P('col'), may hold values from 0.099609375 to 1.8984375
- ln_bias: bfloat16 [12288], P('col'), may hold values from -3 to 3
- weight: bfloat16 [12288, 18432], P('row', 'col'), may hold values from -0.0546875 to 0.0546875
Outputs:
- projected: bfloat16 [4096, 18432], P('row', 'col')
The draws below stay inside these ranges and needn't reach their ends.
All inputs are finite; a program needn't handle non-finite values.
Results may differ from the reference program's by a relative error of at most 0.0049.
Values may be sent and summed in bfloat16 or wider, within the bound.
A program may use at most 128 MiB of HBM per device.

```python
import math
import jax
import jax.numpy as jnp
from jax import lax

D = 12288
OUT = 18432
TOKENS = 4096


def draw_tokens(key, part):
    key = jax.random.fold_in(key, 7)
    first, second, third = jax.random.split(key, 3)
    base = jnp.clip(jax.random.normal(first, (TOKENS, D), jnp.float32), -6.0, 6.0)
    rows = jnp.exp(jax.random.uniform(second, (TOKENS, 1), jnp.float32) * math.log(10.0))
    ramp = jnp.exp(jnp.arange(D, dtype=jnp.float32) / D * math.log(3.0))
    cols = ramp * jnp.exp(jax.random.uniform(third, (D,), jnp.float32) * math.log(2.0))
    values = jnp.clip(base * rows * cols, -500.0, 500.0)
    return values.astype(jnp.bfloat16)


def block_levels(stream_key, dims, cuts, low, top_value):
    gain, own = 1.0, jax.random.fold_in(stream_key, 6)
    for axis_at, blocks in cuts:
        steps = jnp.exp(jax.random.uniform(jax.random.fold_in(own, axis_at), (blocks,), jnp.float32, low / len(cuts), top_value / len(cuts)))
        gain = gain * jnp.repeat(steps, dims[axis_at] // blocks).reshape([-1 if axis == axis_at else 1 for axis in range(len(dims))])
    return gain


def gaussian(stream_key, dims, spread, reach, cuts=(), kind=jnp.bfloat16):
    loudness = block_levels(stream_key, dims, cuts, -0.22, 0.18) if cuts else 1.0
    values = jax.random.normal(stream_key, dims, jnp.float32) * spread * loudness
    return jnp.minimum(jnp.maximum(values, -reach), reach).astype(kind)


def setup_inputs(seed: int = 0) -> dict:
    key_list = jax.random.split(jax.random.key(seed), 5)
    tokens = draw_tokens(jax.random.fold_in(key_list[4], 71), 0)
    ln_gain = jnp.clip(1.0 + 0.18 * jax.random.normal(key_list[1], (D,), jnp.float32), 0.099609375, 1.8984375).astype(jnp.bfloat16)
    ln_bias = gaussian(key_list[2], (D,), 0.5, 3.0, ((0, 16),))
    weight = gaussian(key_list[3], (D, OUT), D ** -0.5, 0.0546875, ((0, 16), (1, 16)))
    return dict(tokens=tokens, ln_gain=ln_gain, ln_bias=ln_bias, weight=weight)


def reference(tokens, ln_gain, ln_bias, weight):
    values = tokens.astype(jnp.float32)
    mean = lax.optimization_barrier(jnp.sum(values, axis=1)) / D
    var = lax.optimization_barrier(jnp.sum(values * values, axis=1)) / D - mean * mean
    scale = lax.rsqrt(var + 1e-05)
    normed = ((values - mean[:, None]) * scale[:, None] * ln_gain.astype(jnp.float32) + ln_bias.astype(jnp.float32)).astype(jnp.bfloat16)
    return jnp.dot(normed, weight, preferred_element_type=jnp.float32).astype(jnp.bfloat16)
```

```python
import jax
import jax.numpy as jnp
from jax import lax
from jax.experimental import pallas as pl
from jax.experimental.pallas import tpu as pltpu
from jax.sharding import PartitionSpec as P

MESH = pl.DeviceIdType.MESH
D = 12288
TOK, FEAT, COLS = 256, 768, 1152
PIECE = 128
HALF = FEAT // 2
CHUNKS = ((0, 384), (384, 384), (768, 384))
NC = len(CHUNKS)
YN, ZN, XN = 4, 8, 4
SUB = 256


def kernel(tok, gain, bias, w, out, xs, relay, nm, wb0, wb1, wb2, tiles, stat, acc, rs_send, rs_recv,
           bx_s, ax_s, v0_r, v1_r, rl_r, zs_s, zs_r, ys_s, ys_r, dd_s, dd_r, lw_s, tz_s, tz_r, tx_s, tx_r, rs_s, rs_r):
    wb = (wb0, wb1, wb2)
    row, col = lax.axis_index("row"), lax.axis_index("col")
    core, y, x_lo = row % 2, (row // 2) % YN, row // 8
    z, x_hi = col % ZN, col // ZN
    x = 2 * x_hi + x_lo

    def at(x_hi=x_hi, x_lo=x_lo, y=y, z=z, core=core):
        return ((x_lo * YN + y) * 2 + core, x_hi * ZN + z)

    up, down = at(z=(z + 1) % ZN), at(z=(z + ZN - 1) % ZN)
    fore, back = at(y=(y + 1) % YN), at(y=(y + YN - 1) % YN)
    near = at(x_lo=1 - x_lo)
    over = at(x_hi=1 - x_hi, x_lo=1 - x_lo)
    opp = at(x_hi=1 - x_hi)
    twin = at(core=1 - core)
    zpeer = [None] + [at(z=(z + k) % ZN) for k in range(1, ZN)]
    xpeer = [None, near, over, opp]
    edge = x_lo == x_hi

    def send(src, dst, ssem, rsem, where):
        return pltpu.make_async_remote_copy(src_ref=src, dst_ref=dst, send_sem=ssem, recv_sem=rsem, device_id=where,
                                            device_id_type=MESH)

    barrier = pltpu.get_barrier_semaphore()
    partners = [*zpeer[1:], *xpeer[1:], fore, back, twin]
    for where in partners:
        pl.semaphore_signal(barrier, inc=1, device_id=where, device_id_type=MESH)
    pl.semaphore_wait(barrier, len(partners))

    def y_rows(dirn, k):
        half = (0, 1, 0)[k] if dirn == 0 else (1, 0, 1)[k]
        return pl.ds(half * HALF, HALF)

    def y_copy(dirn, c, k, arriving=False):
        hops = (1 if arriving else 0) + (1 if k == 2 else 0)
        owner = (y + YN - hops) % YN if dirn == 0 else (y + hops) % YN
        rows = y_rows(dirn, k)
        dst = wb[c].at[2 * owner + core, rows]
        src = dst
        if k < 2 and not arriving:
            start, size = CHUNKS[c]
            src = w.at[rows, pl.ds(start, size)]
        return send(src, dst, ys_s.at[dirn, c * 3 + k], ys_r.at[dirn, c * 3 + k], fore if dirn == 0 else back)

    def d_copy(c, i, arriving=False):
        owner = (y, (y + YN - 1) % YN, (y + 1) % YN, (y + 2) % YN)[i]
        dst = wb[c].at[2 * owner + ((1 - core) if arriving else core)]
        src = dst
        if i == 0 and not arriving:
            start, size = CHUNKS[c]
            src = w.at[:, pl.ds(start, size)]
        return send(src, dst, dd_s.at[c * 4 + i], dd_r.at[c * 4 + i], twin)

    def own_w(c):
        start, size = CHUNKS[c]
        return pltpu.make_async_copy(w.at[:, pl.ds(start, size)], wb[c].at[2 * y + core], lw_s.at[c])

    def rows_of(p):
        return pl.ds(p * PIECE, PIECE)

    def z_copy(dirn, v, s, p, arriving=False):
        hops = s + (1 if arriving else 0)
        block = (z + ZN - hops) % ZN if dirn == 0 else (z + hops) % ZN
        ref = xs.at[block, v, rows_of(p)]
        k = v * 8 + s * 2 + p
        return send(ref, ref, zs_s.at[dirn, k], zs_r.at[dirn, k], up if dirn == 0 else down)

    def to_over(p, edge_case):
        dst = relay.at[rows_of(p)] if edge_case else xs.at[z, 0, rows_of(p)]
        return send(tok.at[rows_of(p)], dst, bx_s.at[p], (rl_r if edge_case else v0_r).at[p], over)

    def to_near(p, edge_case):
        src = relay.at[rows_of(p)] if edge_case else tok.at[rows_of(p)]
        dst = xs.at[z, 1 if edge_case else 0, rows_of(p)]
        return send(src, dst, ax_s.at[p], (v1_r if edge_case else v0_r).at[p], near)

    def keep(p):
        return pltpu.make_async_copy(tok.at[rows_of(p)], xs.at[z, 1, rows_of(p)], v1_r.at[p])

    @pl.when(edge)
    def _():
        for p in range(2):
            to_over(p, True).start()
            keep(p).start()

    @pl.when(jnp.logical_not(edge))
    def _():
        for p in range(2):
            to_over(p, False).start()
            to_near(p, False).start()

    for k in range(2):
        for dirn in range(2):
            y_copy(dirn, 0, k).start()
    d_copy(0, 0).start()
    for c in range(NC):
        own_w(c).start()

    ones = jnp.ones((8, FEAT), jnp.bfloat16)
    over_lanes = (((1,), (1,)), ((), ()))
    values = tok[...]
    wide = values.astype(jnp.float32)
    square = wide * wide
    high = square.astype(jnp.bfloat16)
    low = (square - high.astype(jnp.float32)).astype(jnp.bfloat16)
    total = lax.dot_general(ones, values, over_lanes, preferred_element_type=jnp.float32)
    squares = lax.dot_general(ones, high, over_lanes, preferred_element_type=jnp.float32)
    squares += lax.dot_general(ones, low, over_lanes, preferred_element_type=jnp.float32)
    tiles[x, z, 0:1] = total[0:1]
    tiles[x, z, 1:2] = squares[0:1]
    for j in range(3):
        tiles[x, z, 2 + j:3 + j] = gain[:, j * SUB:(j + 1) * SUB].astype(jnp.float32)
        tiles[x, z, 5 + j:6 + j] = bias[:, j * SUB:(j + 1) * SUB].astype(jnp.float32)

    def tile_z(k):
        return send(tiles.at[x, z], tiles.at[x, z], tz_s.at[k], tz_r.at[k], zpeer[k])

    def tile_z_in(k):
        ref = tiles.at[x, (z + ZN - k) % ZN]
        return send(ref, ref, tz_s.at[k], tz_r.at[k], zpeer[k])

    x_of = (x, 2 * x_hi + 1 - x_lo, 2 * (1 - x_hi) + 1 - x_lo, 2 * (1 - x_hi) + x_lo)

    def tile_x(k, arriving=False):
        ref = tiles.at[x_of[k] if arriving else x]
        return send(ref, ref, tx_s.at[k], tx_r.at[k], xpeer[k])

    for k in range(1, ZN):
        tile_z(k).start()
    for k in range(1, ZN):
        tile_z_in(k).wait_recv()
    for k in range(1, XN):
        tile_x(k).start()

    def z_first(v, p):
        for dirn in range(2):
            z_copy(dirn, v, 0, p).start()

    def v0_arrive(p):
        to_near(p, False).wait_recv()

    def v1_arrive(p):
        to_near(p, True).wait_recv()

    def relay_on(p):
        @pl.when(edge)
        def _():
            to_over(p, True).wait_recv()
            to_near(p, True).start()

    def y_tick(c, k):
        for dirn in range(2):
            y_copy(dirn, c, k, arriving=True).wait_recv()
        if k == 0:
            for dirn in range(2):
                y_copy(dirn, c, 2).start()
        if k < 2 and c + 1 < NC:
            for dirn in range(2):
                y_copy(dirn, c + 1, k).start()
        if k == 1:
            d_copy(c, 1).start()
            d_copy(c, 2).start()
            if c + 1 < NC:
                d_copy(c + 1, 0).start()
        if k == 2:
            d_copy(c, 3).start()

    def normalize(block, v, p):
        lanes = 2 * v
        mean = stat[p * PIECE:(p + 1) * PIECE, lanes:lanes + 1]
        scale = stat[p * PIECE:(p + 1) * PIECE, lanes + 1:lanes + 2]
        for j in range(3):
            g = tiles[2 * x_lo, block, 2 + j:3 + j]
            b = tiles[2 * x_lo, block, 5 + j:6 + j]
            part = xs[block, v, p * PIECE:(p + 1) * PIECE, j * SUB:(j + 1) * SUB].astype(jnp.float32)
            nm[v, block, p * PIECE:(p + 1) * PIECE, j * SUB:(j + 1) * SUB] = (
                (part - mean) * scale * g + b).astype(jnp.bfloat16)

    def z_tick(v, s, p):
        arrivals = []
        if s < 3:
            arrivals = [0, 1]
        elif p == 0:
            arrivals = [0]
        else:
            arrivals = [1]
        for dirn in arrivals:
            z_copy(dirn, v, s, p, arriving=True).wait_recv()
            if s < 2 or (s == 2 and p == dirn):
                z_copy(dirn, v, s + 1, p).start()
        for dirn in arrivals:
            block = (z + ZN - s - 1) % ZN if dirn == 0 else (z + s + 1) % ZN
            normalize(block, v, p)

    def product(v, c):
        size = CHUNKS[c][1]
        acc[:, :size] = jnp.dot(nm[v, 0], wb[c][0], preferred_element_type=jnp.float32)

        def add(k, carry):
            acc[:, :size] += jnp.dot(nm[v, k], wb[c][k], preferred_element_type=jnp.float32)
            return carry

        lax.fori_loop(1, 2 * YN, add, 0)

    def rs(c):
        start, size = CHUNKS[c]
        cols = pl.ds(start, size)
        return send(rs_send.at[:, cols], rs_recv.at[:, cols], rs_s.at[c], rs_r.at[c], near)

    def give(c):
        start, size = CHUNKS[c]
        product(0, c)
        rs_send[:, start:start + size] = acc[:, :size].astype(jnp.bfloat16)
        rs(c).start()

    def finish(c):
        start, size = CHUNKS[c]
        product(1, c)
        rs(c).wait_recv()
        out[:, start:start + size] = (acc[:, :size] + rs_recv[:, start:start + size].astype(jnp.float32)).astype(jnp.bfloat16)

    def weights_ready(c):
        own_w(c).wait()
        for i in range(4):
            d_copy(c, i, arriving=True).wait_recv()

    v0_arrive(0)
    z_first(0, 0)
    relay_on(0)
    y_tick(0, 0)
    v0_arrive(1)
    z_first(0, 1)
    for k in range(1, XN):
        tile_x(k, arriving=True).wait_recv()
    means = []
    for lo in (1 - x_lo, x_lo):
        sums = jnp.zeros((8, SUB), jnp.float32)
        for hi in range(2):
            for zz in range(ZN):
                sums += tiles[2 * hi + lo, zz]
        mean = sums[0:1] / D
        var = sums[1:2] / D - mean * mean
        means += [mean, lax.rsqrt(var + 1e-05)]
    rows = jnp.concatenate(means + [jnp.zeros((124, SUB), jnp.float32)], axis=0)
    stat[...] = rows.T
    relay_on(1)
    for p in range(2):
        normalize(z, 0, p)
    y_tick(0, 1)
    z_tick(0, 0, 0)
    z_tick(0, 0, 1)
    z_tick(0, 1, 0)
    y_tick(0, 2)
    z_tick(0, 1, 1)
    y_tick(1, 0)
    v1_arrive(0)
    z_tick(0, 2, 0)
    z_first(1, 0)
    v1_arrive(1)
    z_tick(0, 2, 1)
    z_first(1, 1)
    y_tick(1, 1)
    z_tick(0, 3, 0)
    z_tick(0, 3, 1)
    for p in range(2):
        normalize(z, 1, p)
    weights_ready(0)
    give(0)
    y_tick(1, 2)
    z_tick(1, 0, 0)
    z_tick(1, 0, 1)
    y_tick(2, 0)
    weights_ready(1)
    give(1)
    z_tick(1, 1, 0)
    y_tick(2, 1)
    z_tick(1, 1, 1)
    z_tick(1, 2, 0)
    y_tick(2, 2)
    z_tick(1, 2, 1)
    weights_ready(2)
    give(2)
    z_tick(1, 3, 0)
    z_tick(1, 3, 1)
    for c in range(NC):
        finish(c)

    for p in range(2):
        to_over(p, False).wait_send()
        to_near(p, False).wait_send()
    for k in range(1, ZN):
        tile_z(k).wait_send()
    for k in range(1, XN):
        tile_x(k).wait_send()
    for dirn in range(2):
        for v in range(2):
            for s in range(4):
                for p in range(2):
                    if s < 3 or p == dirn:
                        z_copy(dirn, v, s, p).wait_send()
        for c in range(NC):
            for k in range(3):
                y_copy(dirn, c, k).wait_send()
    for c in range(NC):
        for i in range(4):
            d_copy(c, i).wait_send()
        rs(c).wait_send()


def on_device(tokens, ln_gain, ln_bias, weight):
    vmem = pl.BlockSpec(memory_space=pltpu.VMEM)
    hbm = pl.BlockSpec(memory_space=pl.ANY)
    dma = pltpu.SemaphoreType.DMA
    return pl.pallas_call(
        kernel,
        out_shape=jax.ShapeDtypeStruct((TOK, COLS), jnp.bfloat16),
        in_specs=[vmem, vmem, vmem, hbm],
        out_specs=vmem,
        scratch_shapes=[
            pltpu.VMEM((ZN, 2, TOK, FEAT), jnp.bfloat16),
            pltpu.VMEM((TOK, FEAT), jnp.bfloat16),
            pltpu.VMEM((2, ZN, TOK, FEAT), jnp.bfloat16),
            *[pltpu.VMEM((2 * YN, FEAT, size), jnp.bfloat16) for _, size in CHUNKS],
            pltpu.VMEM((XN, ZN, 8, SUB), jnp.float32),
            pltpu.VMEM((TOK, 128), jnp.float32),
            pltpu.VMEM((TOK, max(size for _, size in CHUNKS)), jnp.float32),
            pltpu.VMEM((TOK, COLS), jnp.bfloat16),
            pltpu.VMEM((TOK, COLS), jnp.bfloat16),
            dma((2,)), dma((2,)), dma((2,)), dma((2,)), dma((2,)),
            dma((2, 16)), dma((2, 16)),
            dma((2, 3 * NC)), dma((2, 3 * NC)),
            dma((4 * NC,)), dma((4 * NC,)),
            dma((NC,)),
            dma((ZN,)), dma((ZN,)), dma((XN,)), dma((XN,)),
            dma((NC,)), dma((NC,)),
        ],
        compiler_params=pltpu.CompilerParams(collective_id=0, has_side_effects=True, vmem_limit_bytes=56 * 1024 * 1024),
        cost_estimate=pl.CostEstimate(flops=2 * TOK * D * COLS, bytes_accessed=4 * 1024 * 1024, transcendentals=0),
    )(tokens, ln_gain.reshape(1, FEAT), ln_bias.reshape(1, FEAT), weight)


def solution(mesh):
    in_specs = (P("row", "col"), P("col"), P("col"), P("row", "col"))
    return jax.shard_map(on_device, mesh=mesh, in_specs=in_specs, out_specs=P("row", "col"), check_vma=False)
```

```python
import jax
import jax.numpy as jnp
from jax import lax
from jax.experimental import pallas as pl
from jax.experimental.pallas import tpu as pltpu
from jax.sharding import PartitionSpec as P

MESH = pl.DeviceIdType.MESH
D = 12288
TOK, FEAT, COLS = 256, 768, 1152
PIECES = (4, 2)
HALF = FEAT // 2
CHUNKS = ((0, 512), (512, 256), (768, 256), (1024, 128))
NC = len(CHUNKS)
YN, ZN, XN = 4, 8, 4
SUB = 256


def kernel(tok, gain, bias, w, out, xs, relay, nm, wb0, wb1, wb2, wb3, tiles, stat, acc, rs_send, rs_recv,
           bx_s, ax_s, v0_r, v1_r, rl_r, zs_s, zs_r, ys_s, ys_r, dd_s, dd_r, lw_s, tz_s, tz_r, tx_s, tx_r, rs_s, rs_r):
    wb = (wb0, wb1, wb2, wb3)
    row, col = lax.axis_index("row"), lax.axis_index("col")
    core, y, x_lo = row % 2, (row // 2) % YN, row // 8
    z, x_hi = col % ZN, col // ZN
    x = 2 * x_hi + x_lo

    def at(x_hi=x_hi, x_lo=x_lo, y=y, z=z, core=core):
        return ((x_lo * YN + y) * 2 + core, x_hi * ZN + z)

    up, down = at(z=(z + 1) % ZN), at(z=(z + ZN - 1) % ZN)
    fore, back = at(y=(y + 1) % YN), at(y=(y + YN - 1) % YN)
    near = at(x_lo=1 - x_lo)
    over = at(x_hi=1 - x_hi, x_lo=1 - x_lo)
    opp = at(x_hi=1 - x_hi)
    twin = at(core=1 - core)
    zpeer = [None] + [at(z=(z + k) % ZN) for k in range(1, ZN)]
    xpeer = [None, near, over, opp]
    edge = x_lo == x_hi

    def send(src, dst, ssem, rsem, where):
        return pltpu.make_async_remote_copy(src_ref=src, dst_ref=dst, send_sem=ssem, recv_sem=rsem, device_id=where,
                                            device_id_type=MESH)

    barrier = pltpu.get_barrier_semaphore()
    partners = [*zpeer[1:], *xpeer[1:], fore, back, twin]
    for where in partners:
        pl.semaphore_signal(barrier, inc=1, device_id=where, device_id_type=MESH)
    pl.semaphore_wait(barrier, len(partners))

    def slot(y, core):
        rel = (2 * y + core + ZN - z) % ZN
        return 2 * rel + (rel // 4) * (15 - 4 * rel)

    def block_rows(y, core, start=0, size=FEAT):
        return pl.ds(pl.multiple_of(slot(y, core) * FEAT + start, 128), size)

    def y_copy(dirn, c, k, arriving=False):
        hops = (1 if arriving else 0) + (1 if k == 2 else 0)
        owner = (y + YN - hops) % YN if dirn == 0 else (y + hops) % YN
        half = ((0, 1, 0)[k] if dirn == 0 else (1, 0, 1)[k]) * HALF
        dst = wb[c].at[block_rows(owner, core, half, HALF)]
        src = dst
        if k < 2 and not arriving:
            start, size = CHUNKS[c]
            src = w.at[pl.ds(half, HALF), pl.ds(start, size)]
        return send(src, dst, ys_s.at[dirn, c * 3 + k], ys_r.at[dirn, c * 3 + k], fore if dirn == 0 else back)

    def d_copy(c, i, arriving=False):
        owner = (y, (y + YN - 1) % YN, (y + 1) % YN, (y + 2) % YN)[i]
        dst = wb[c].at[block_rows(owner, (1 - core) if arriving else core)]
        src = dst
        if i == 0 and not arriving:
            start, size = CHUNKS[c]
            src = w.at[:, pl.ds(start, size)]
        return send(src, dst, dd_s.at[c * 4 + i], dd_r.at[c * 4 + i], twin)

    def own_w(c):
        start, size = CHUNKS[c]
        return pltpu.make_async_copy(w.at[:, pl.ds(start, size)], wb[c].at[block_rows(y, core)], lw_s.at[c])

    def rows_of(v, p):
        size = TOK // PIECES[v]
        return pl.ds(p * size, size)

    def z_copy(dirn, v, s, p, arriving=False):
        hops = s + (1 if arriving else 0)
        block = (z + ZN - hops) % ZN if dirn == 0 else (z + hops) % ZN
        ref = xs.at[block, v, rows_of(v, p)]
        k = v * 16 + s * PIECES[v] + p
        return send(ref, ref, zs_s.at[dirn, k], zs_r.at[dirn, k], up if dirn == 0 else down)

    def to_over(p, edge_case):
        rows = rows_of(1 if edge_case else 0, p)
        dst = relay.at[rows] if edge_case else xs.at[z, 0, rows]
        return send(tok.at[rows], dst, bx_s.at[p], (rl_r if edge_case else v0_r).at[p], over)

    def to_near(p, edge_case):
        rows = rows_of(1 if edge_case else 0, p)
        src = relay.at[rows] if edge_case else tok.at[rows]
        dst = xs.at[z, 1 if edge_case else 0, rows]
        return send(src, dst, ax_s.at[p], (v1_r if edge_case else v0_r).at[p], near)

    def keep(p):
        rows = rows_of(1, p)
        return pltpu.make_async_copy(tok.at[rows], xs.at[z, 1, rows], v1_r.at[p])

    @pl.when(edge)
    def _():
        for p in range(PIECES[1]):
            to_over(p, True).start()
            keep(p).start()

    @pl.when(jnp.logical_not(edge))
    def _():
        for p in range(PIECES[0]):
            to_over(p, False).start()
            to_near(p, False).start()

    def y_own(c, k):
        for dirn in range(2):
            y_copy(dirn, c, k).start()

    y_own(0, 0)
    y_own(0, 1)
    y_own(1, 0)
    for c in range(NC):
        d_copy(c, 0).start()
        own_w(c).start()

    ones = jnp.ones((8, FEAT), jnp.bfloat16)
    over_lanes = (((1,), (1,)), ((), ()))
    values = tok[...]
    wide = values.astype(jnp.float32)
    square = wide * wide
    high = square.astype(jnp.bfloat16)
    low = (square - high.astype(jnp.float32)).astype(jnp.bfloat16)
    total = lax.dot_general(ones, values, over_lanes, preferred_element_type=jnp.float32)
    squares = lax.dot_general(ones, high, over_lanes, preferred_element_type=jnp.float32)
    squares += lax.dot_general(ones, low, over_lanes, preferred_element_type=jnp.float32)
    tiles[x, z, 0:1] = total[0:1]
    tiles[x, z, 1:2] = squares[0:1]
    for j in range(3):
        tiles[x, z, 2 + j:3 + j] = gain[j * SUB:(j + 1) * SUB].astype(jnp.float32).reshape(1, SUB)
        tiles[x, z, 5 + j:6 + j] = bias[j * SUB:(j + 1) * SUB].astype(jnp.float32).reshape(1, SUB)

    def tile_z(k):
        return send(tiles.at[x, z], tiles.at[x, z], tz_s.at[k], tz_r.at[k], zpeer[k])

    def tile_z_in(k):
        ref = tiles.at[x, (z + ZN - k) % ZN]
        return send(ref, ref, tz_s.at[k], tz_r.at[k], zpeer[k])

    x_of = (x, 2 * x_hi + 1 - x_lo, 2 * (1 - x_hi) + 1 - x_lo, 2 * (1 - x_hi) + x_lo)

    def tile_x(k, arriving=False):
        ref = tiles.at[x_of[k] if arriving else x]
        return send(ref, ref, tx_s.at[k], tx_r.at[k], xpeer[k])

    for k in range(1, ZN):
        tile_z(k).start()

    def z_first(v, p):
        for dirn in range(2):
            z_copy(dirn, v, 0, p).start()

    def v0_arrive(p):
        to_near(p, False).wait_recv()

    def v1_arrive(p):
        to_near(p, True).wait_recv()

    def relay_on(p):
        @pl.when(edge)
        def _():
            to_over(p, True).wait_recv()
            to_near(p, True).start()

    def y_tick(c, k, own=()):
        for dirn in range(2):
            y_copy(dirn, c, k, arriving=True).wait_recv()
        if k == 0:
            y_own(c, 2)
        for piece in own:
            y_own(*piece)
        if k == 1:
            d_copy(c, 1).start()
            d_copy(c, 2).start()
        if k == 2:
            d_copy(c, 3).start()

    def normalize(v, p, at, block):
        size = TOK // PIECES[v]
        rows = slice(p * size, (p + 1) * size)
        mean, scale = stat[rows, 2 * v:2 * v + 1], stat[rows, 2 * v + 1:2 * v + 2]
        for j in range(3):
            g = tiles[2 * x_lo, block, 2 + j:3 + j]
            b = tiles[2 * x_lo, block, 5 + j:6 + j]
            part = xs[block, v, rows, j * SUB:(j + 1) * SUB].astype(jnp.float32)
            nm[v, rows, at * FEAT + j * SUB:at * FEAT + (j + 1) * SUB] = ((part - mean) * scale * g + b).astype(jnp.bfloat16)

    def last_hop(dirn, v):
        half = PIECES[v] // 2
        return range(half) if dirn == 0 else range(half, 2 * half)

    def z_tick(v, s, p):
        arrivals = [0, 1]
        for dirn in arrivals:
            piece = last_hop(dirn, v)[p] if s == 3 else p
            z_copy(dirn, v, s, piece, arriving=True).wait_recv()
            if s < 2 or (s == 2 and piece in last_hop(dirn, v)):
                z_copy(dirn, v, s + 1, piece).start()
        for dirn in arrivals:
            piece = last_hop(dirn, v)[p] if s == 3 else p
            block = (z + ZN - s - 1) % ZN if dirn == 0 else (z + s + 1) % ZN
            normalize(v, piece, 7 if s == 3 else 2 * s + 1 + dirn, block)

    def product(v, c, first, last):
        k = slice(first * FEAT, last * FEAT)
        return jnp.dot(nm[v, :, k], wb[c][k], preferred_element_type=jnp.float32)

    def cols(c):
        start, size = CHUNKS[c]
        return slice(start, start + size)

    def rs(c):
        at = pl.ds(*CHUNKS[c])
        return send(rs_send.at[:, at], rs_recv.at[:, at], rs_s.at[c], rs_r.at[c], near)

    def give(c):
        own_w(c).wait()
        for i in range(4):
            d_copy(c, i, arriving=True).wait_recv()
        rs_send[:, cols(c)] = product(0, c, 0, ZN).astype(jnp.bfloat16)
        rs(c).start()

    for p in range(PIECES[0]):
        v0_arrive(p)
        z_first(0, p)
        if p == 1:
            for k in range(1, ZN):
                tile_z_in(k).wait_recv()
            for k in range(1, XN):
                tile_x(k).start()
            relay_on(0)
    for k in range(1, XN):
        tile_x(k, arriving=True).wait_recv()
    means = []
    for lo in (1 - x_lo, x_lo):
        sums = jnp.zeros((8, SUB), jnp.float32)
        for hi in range(2):
            for zz in range(ZN):
                sums += tiles[2 * hi + lo, zz]
        mean = sums[0:1] / D
        var = sums[1:2] / D - mean * mean
        means += [mean, lax.rsqrt(var + 1e-05)]
    stat[...] = jnp.concatenate(means + [jnp.zeros((124, SUB), jnp.float32)], axis=0).T
    z_tick(0, 0, 0)
    relay_on(1)
    z_tick(0, 0, 1)
    y_tick(0, 0, [(1, 1)])
    z_tick(0, 0, 2)
    z_tick(0, 0, 3)
    for p in range(PIECES[0]):
        normalize(0, p, 0, z)
    z_tick(0, 1, 0)
    z_tick(0, 1, 1)
    y_tick(0, 1, [(2, 0)])
    z_tick(0, 1, 2)
    z_tick(0, 1, 3)
    y_tick(1, 0, [(2, 1)])
    z_tick(0, 2, 0)
    z_tick(0, 2, 1)
    v1_arrive(0)
    z_first(1, 0)
    z_tick(0, 2, 2)
    z_tick(0, 2, 3)
    v1_arrive(1)
    z_first(1, 1)
    y_tick(0, 2, [(3, 0)])
    z_tick(0, 3, 0)
    z_tick(0, 3, 1)
    y_tick(1, 1, [(3, 1)])
    give(0)
    for p in range(PIECES[1]):
        normalize(1, p, 0, z)
    z_tick(1, 0, 0)
    y_tick(2, 0)
    z_tick(1, 0, 1)
    y_tick(1, 2)
    give(1)
    z_tick(1, 1, 0)
    y_tick(2, 1)
    y_tick(3, 0)
    z_tick(1, 1, 1)
    y_tick(3, 1)
    for c in range(2):
        acc[:, cols(c)] = product(1, c, 0, 5)
    z_tick(1, 2, 0)
    y_tick(2, 2)
    give(2)
    y_tick(3, 2)
    give(3)
    z_tick(1, 2, 1)
    for c in range(2):
        acc[:, cols(c)] += product(1, c, 5, 7)
    for c in range(2, NC):
        acc[:, cols(c)] = product(1, c, 0, 7)
    z_tick(1, 3, 0)
    for c in range(NC):
        rs(c).wait_recv()
        own = acc[:, cols(c)] + product(1, c, 7, ZN)
        out[:, cols(c)] = (own + rs_recv[:, cols(c)].astype(jnp.float32)).astype(jnp.bfloat16)

    @pl.when(edge)
    def _():
        for p in range(PIECES[1]):
            to_over(p, True).wait_send()
            to_near(p, True).wait_send()

    @pl.when(jnp.logical_not(edge))
    def _():
        for p in range(PIECES[0]):
            to_over(p, False).wait_send()
            to_near(p, False).wait_send()

    for k in range(1, ZN):
        tile_z(k).wait_send()
    for k in range(1, XN):
        tile_x(k).wait_send()
    for dirn in range(2):
        for v in range(2):
            for s in range(4):
                for p in range(PIECES[v]):
                    if s < 3 or p in last_hop(dirn, v):
                        z_copy(dirn, v, s, p).wait_send()
        for c in range(NC):
            for k in range(3):
                y_copy(dirn, c, k).wait_send()
    for c in range(NC):
        for i in range(4):
            d_copy(c, i).wait_send()
        rs(c).wait_send()


def on_device(tokens, ln_gain, ln_bias, weight):
    vmem = pl.BlockSpec(memory_space=pltpu.VMEM)
    hbm = pl.BlockSpec(memory_space=pl.ANY)
    dma = pltpu.SemaphoreType.DMA
    return pl.pallas_call(
        kernel,
        out_shape=jax.ShapeDtypeStruct((TOK, COLS), jnp.bfloat16),
        in_specs=[vmem, vmem, vmem, hbm],
        out_specs=vmem,
        scratch_shapes=[
            pltpu.VMEM((ZN, 2, TOK, FEAT), jnp.bfloat16),
            pltpu.VMEM((TOK, FEAT), jnp.bfloat16),
            pltpu.VMEM((2, TOK, ZN * FEAT), jnp.bfloat16),
            *[pltpu.VMEM((ZN * FEAT, size), jnp.bfloat16) for _, size in CHUNKS],
            pltpu.VMEM((XN, ZN, 8, SUB), jnp.float32),
            pltpu.VMEM((TOK, 128), jnp.float32),
            pltpu.VMEM((TOK, COLS), jnp.float32),
            pltpu.VMEM((TOK, COLS), jnp.bfloat16),
            pltpu.VMEM((TOK, COLS), jnp.bfloat16),
            dma((4,)), dma((4,)), dma((4,)), dma((2,)), dma((2,)),
            dma((2, 24)), dma((2, 24)),
            dma((2, 3 * NC)), dma((2, 3 * NC)),
            dma((4 * NC,)), dma((4 * NC,)),
            dma((NC,)),
            dma((ZN,)), dma((ZN,)), dma((XN,)), dma((XN,)),
            dma((NC,)), dma((NC,)),
        ],
        compiler_params=pltpu.CompilerParams(collective_id=0, has_side_effects=True, vmem_limit_bytes=58 * 1024 * 1024),
        cost_estimate=pl.CostEstimate(flops=2 * TOK * D * COLS, bytes_accessed=4 * 1024 * 1024, transcendentals=0),
    )(tokens, ln_gain, ln_bias, weight)


def solution(mesh):
    in_specs = (P("row", "col"), P("col"), P("col"), P("row", "col"))
    return jax.shard_map(on_device, mesh=mesh, in_specs=in_specs, out_specs=P("row", "col"), check_vma=False)
```

```python
import jax
import jax.numpy as jnp
from jax import lax
from jax.experimental import pallas as pl
from jax.experimental.pallas import tpu as pltpu
from jax.sharding import PartitionSpec as P

MESH = pl.DeviceIdType.MESH
D = 12288
TOK, FEAT, COLS = 256, 768, 1152
EARLY = 96
PIECES = (2, 2)
HALF = FEAT // 2
CHUNKS = ((0, 512), (512, 256), (768, 256), (1024, 128))
NC = len(CHUNKS)
YN, ZN, XN = 4, 8, 4
SUB = 256


def kernel(tok_in, gain, bias, w, out, xs, relay, zb, nm, wb0, wb1, wb2, wb3, tiles, stat, acc, ahead, result, tok, rs_send, rs_recv,
           bx_s, ax_s, v0_r, v1_r, rl_r, zs_s, zs_r, ys_s, ys_r, dd_s, dd_r, lw_s, tz_s, tz_r, tx_s, tx_r, rs_s, rs_r,
           er_s, er_r, eo_s, eo_r, en_s, en_r, out_s, tok_s):
    wb = (wb0, wb1, wb2, wb3)
    row, col = lax.axis_index("row"), lax.axis_index("col")
    core, y, x_lo = row % 2, (row // 2) % YN, row // 8
    z, x_hi = col % ZN, col // ZN
    x = 2 * x_hi + x_lo

    def at(x_hi=x_hi, x_lo=x_lo, y=y, z=z, core=core):
        return ((x_lo * YN + y) * 2 + core, x_hi * ZN + z)

    up, down = at(z=(z + 1) % ZN), at(z=(z + ZN - 1) % ZN)
    fore, back = at(y=(y + 1) % YN), at(y=(y + YN - 1) % YN)
    near = at(x_lo=1 - x_lo)
    over = at(x_hi=1 - x_hi, x_lo=1 - x_lo)
    twin = at(core=1 - core)
    edge = x_lo == x_hi
    edge_index = (x_lo + x_hi + 1) % 2

    def send(src, dst, ssem, rsem, where):
        return pltpu.make_async_remote_copy(src_ref=src, dst_ref=dst, send_sem=ssem, recv_sem=rsem, device_id=where,
                                            device_id_type=MESH)

    def slot(y, core):
        rel = (2 * y + core + ZN - z) % ZN
        return 2 * rel + (rel // 4) * (15 - 4 * rel)

    def block_rows(y, core, start=0, size=FEAT):
        return pl.ds(pl.multiple_of(slot(y, core) * FEAT + start, 128), size)

    tokens_in = pltpu.make_async_copy(tok_in, tok, tok_s)
    tokens_in.start()

    barrier = pltpu.get_barrier_semaphore()
    partners = [fore, back, near, over, twin] + [at(z=(z + k) % ZN) for k in range(1, ZN)]
    for where in partners:
        pl.semaphore_signal(barrier, inc=1, device_id=where, device_id_type=MESH)

    def own_w(c):
        start, size = CHUNKS[c]
        return pltpu.make_async_copy(w.at[:, pl.ds(start, size)], wb[c].at[block_rows(y, core)], lw_s.at[c])

    for c in range(NC):
        own_w(c).start()
    tokens_in.wait()
    zb[0, z] = tok[:EARLY]

    ones = jnp.ones((8, FEAT), jnp.bfloat16)
    over_lanes = (((1,), (1,)), ((), ()))
    values = tok[...]
    wide = values.astype(jnp.float32)
    square = wide * wide
    high = square.astype(jnp.bfloat16)
    low = (square - high.astype(jnp.float32)).astype(jnp.bfloat16)
    total = lax.dot_general(ones, values, over_lanes, preferred_element_type=jnp.float32)
    squares = lax.dot_general(ones, high, over_lanes, preferred_element_type=jnp.float32)
    squares += lax.dot_general(ones, low, over_lanes, preferred_element_type=jnp.float32)
    tiles[x, z, 0:1] = total[0:1]
    tiles[x, z, 1:2] = squares[0:1]
    for j in range(3):
        tiles[x, z, 2 + j:3 + j] = gain[j * SUB:(j + 1) * SUB].astype(jnp.float32).reshape(1, SUB)
        tiles[x, z, 5 + j:6 + j] = bias[j * SUB:(j + 1) * SUB].astype(jnp.float32).reshape(1, SUB)

    pl.semaphore_wait(barrier, len(partners))

    def y_copy(dirn, c, k, arriving=False):
        hops = (1 if arriving else 0) + (1 if k == 2 else 0)
        owner = (y + YN - hops) % YN if dirn == 0 else (y + hops) % YN
        half = ((0, 1, 0)[k] if dirn == 0 else (1, 0, 1)[k]) * HALF
        dst = wb[c].at[block_rows(owner, core, half, HALF)]
        src = dst
        if k < 2 and not arriving:
            start, size = CHUNKS[c]
            src = w.at[pl.ds(half, HALF), pl.ds(start, size)]
        return send(src, dst, ys_s.at[dirn, c * 3 + k], ys_r.at[dirn, c * 3 + k], fore if dirn == 0 else back)

    def d_copy(c, i, arriving=False):
        owner = (y, (y + YN - 1) % YN, (y + 1) % YN, (y + 2) % YN)[i]
        dst = wb[c].at[block_rows(owner, (1 - core) if arriving else core)]
        src = dst
        if i == 0 and not arriving:
            start, size = CHUNKS[c]
            src = w.at[:, pl.ds(start, size)]
        return send(src, dst, dd_s.at[c * 4 + i], dd_r.at[c * 4 + i], twin)

    def rows_of(v, p):
        size = (TOK - EARLY) // PIECES[v]
        return pl.ds(EARLY + p * size, size)

    def z_copy(dirn, v, s, p, arriving=False):
        hops = s + (1 if arriving else 0)
        block = (z + ZN - hops) % ZN if dirn == 0 else (z + hops) % ZN
        ref = xs.at[block, v, rows_of(v, p)]
        k = v * 16 + s * PIECES[v] + p
        return send(ref, ref, zs_s.at[dirn, k], zs_r.at[dirn, k], up if dirn == 0 else down)

    def block_at(i):
        if i == 0:
            return z
        return (z + ZN - (i + 1) // 2) % ZN if i % 2 else (z + i // 2) % ZN

    def early_z(dirn, s, q, arriving=False):
        hops = s + (1 if arriving else 0)
        block = (z + ZN - hops) % ZN if dirn == 0 else (z + hops) % ZN
        ref = zb.at[0, block, pl.ds(q * (EARLY // 2), EARLY // 2)]
        return send(ref, ref, er_s.at[dirn, 2 * s + q], er_r.at[dirn, 2 * s + q], up if dirn == 0 else down)

    def early_over(i):
        block = block_at(i)
        return send(zb.at[0, block], zb.at[1, block], eo_s.at[i], eo_r.at[i], over)

    def early_near(i):
        block = block_at(i)
        return send(zb.at[edge_index, block], zb.at[2, block], en_s.at[i], en_r.at[i], near)

    def early_tick(s):
        for dirn in range(2):
            for q in range(2):
                if s < 3 or q == dirn:
                    early_z(dirn, s, q, arriving=True).wait_recv()
                    if s < 2 or (s == 2 and q == dirn):
                        early_z(dirn, s + 1, q).start()
        for i in (7,) if s == 3 else (2 * s + 1, 2 * s + 2):
            early_over(i).start()

    def early_on(i):
        early_over(i).wait_recv()
        early_near(i).start()

    def to_over(p, edge_case):
        rows = rows_of(1 if edge_case else 0, p)
        dst = relay.at[rows] if edge_case else xs.at[z, 0, rows]
        return send(tok.at[rows], dst, bx_s.at[p], (rl_r if edge_case else v0_r).at[p], over)

    def to_near(p, edge_case):
        rows = rows_of(1 if edge_case else 0, p)
        src = relay.at[rows] if edge_case else tok.at[rows]
        dst = xs.at[z, 1 if edge_case else 0, rows]
        return send(src, dst, ax_s.at[p], (v1_r if edge_case else v0_r).at[p], near)

    def keep(p):
        rows = rows_of(1, p)
        return pltpu.make_async_copy(tok.at[rows], xs.at[z, 1, rows], v1_r.at[p])

    def tile_z(k, arriving=False):
        ref = tiles.at[x, (z + ZN - k) % ZN if arriving else z]
        return send(ref, ref, tz_s.at[k], tz_r.at[k], at(z=(z + k) % ZN))

    def tiles_in():
        for k in range(1, ZN):
            tile_z(k, arriving=True).wait_recv()
        for k in range(2):
            tile_x(k).start()
        early_over(0).start()

    def y_own(c, k):
        for dirn in range(2):
            y_copy(dirn, c, k).start()

    for k in range(1, ZN):
        tile_z(k).start()
    y_own(0, 0)
    @pl.when(edge)
    def _():
        for p in range(PIECES[1]):
            to_over(p, True).start()
            keep(p).start()

    @pl.when(jnp.logical_not(edge))
    def _():
        for p in range(PIECES[0]):
            to_over(p, False).start()
            to_near(p, False).start()

    y_own(0, 1)
    y_own(1, 0)
    for q in range(2):
        for dirn in range(2):
            early_z(dirn, 0, q).start()
    for c in range(NC):
        d_copy(c, 0).start()

    x_near, x_over, x_far = 2 * x_hi + 1 - x_lo, 2 * (1 - x_hi) + 1 - x_lo, 2 * (1 - x_hi) + x_lo

    def tile_x(k, arriving=False):
        ref = tiles.at[(x_near, x_over, x_far)[k] if arriving else (x, x, x_near)[k]]
        return send(ref, ref, tx_s.at[k], tx_r.at[k], near if k == 0 else over)

    def z_first(v, p):
        for dirn in range(2):
            z_copy(dirn, v, 0, p).start()

    def v0_arrive(p):
        to_near(p, False).wait_recv()

    def v1_arrive(p):
        to_near(p, True).wait_recv()

    def relay_on(p):
        @pl.when(edge)
        def _():
            to_over(p, True).wait_recv()
            to_near(p, True).start()

    def y_tick(c, k, own=()):
        for dirn in range(2):
            y_copy(dirn, c, k, arriving=True).wait_recv()
        for piece in own[:1]:
            y_own(*piece)
        if k == 0:
            y_own(c, 2)
        for piece in own[1:]:
            y_own(*piece)
        if k == 1:
            d_copy(c, 1).start()
            d_copy(c, 2).start()
        if k == 2:
            d_copy(c, 3).start()

    def normalize(v, rows, at, block, source):
        mean, scale = stat[rows, 2 * v:2 * v + 1], stat[rows, 2 * v + 1:2 * v + 2]
        for j in range(3):
            lanes = slice(j * SUB, (j + 1) * SUB)
            g = tiles[2 * x_lo, block, 2 + j:3 + j]
            b = tiles[2 * x_lo, block, 5 + j:6 + j]
            part = source[:, lanes].astype(jnp.float32)
            nm[v, rows, at * FEAT + j * SUB:at * FEAT + (j + 1) * SUB] = ((part - mean) * scale * g + b).astype(jnp.bfloat16)

    def normalize_piece(v, p, i):
        size = (TOK - EARLY) // PIECES[v]
        start = EARLY + p * size
        block = block_at(i)
        normalize(v, slice(start, start + size), i, block, xs.at[block, v, pl.ds(start, size)])

    def normalize_early(i):
        block = block_at(i)
        early_near(i).wait_recv()
        normalize(0, slice(0, EARLY), i, block, zb.at[1 + edge_index, block])
        normalize(1, slice(0, EARLY), i, block, zb.at[2 - 2 * edge_index, block])

    def last_hop(dirn, v):
        half = PIECES[v] // 2
        return range(half) if dirn == 0 else range(half, 2 * half)

    def z_move(v, s, p):
        for dirn in range(2):
            piece = last_hop(dirn, v)[p] if s == 3 else p
            z_copy(dirn, v, s, piece, arriving=True).wait_recv()
            if s < 2 or (s == 2 and piece in last_hop(dirn, v)):
                z_copy(dirn, v, s + 1, piece).start()

    def z_norm(v, s, p):
        for dirn in range(2):
            normalize_piece(v, last_hop(dirn, v)[p] if s == 3 else p, 7 if s == 3 else 2 * s + 1 + dirn)

    def product(v, c, first, last):
        k = slice(first * FEAT, last * FEAT)
        return jnp.dot(nm[v, :, k], wb[c][k], preferred_element_type=jnp.float32)

    def product_of(v, c, owners):
        total = None
        for owner in owners:
            for k in range(2):
                at = block_rows((y + owner) % YN, k)
                part = jnp.dot(nm[v, :, at], wb[c][at], preferred_element_type=jnp.float32)
                total = part if total is None else total + part
        return total

    def cols(c):
        start, size = CHUNKS[c]
        return slice(start, start + size)

    def rs(c):
        at = pl.ds(*CHUNKS[c])
        return send(rs_send.at[:, at], rs_recv.at[:, at], rs_s.at[c], rs_r.at[c], near)

    def weights(c, blocks):
        if 0 in blocks:
            own_w(c).wait()
        for i in blocks:
            d_copy(c, i, arriving=True).wait_recv()

    def before(c):
        weights(c, range(3))
        ahead[...] = product_of(0, c, (0, 3, 1))

    def give(c):
        if c == NC - 1:
            weights(c, (3,))
            part = ahead[...] + product_of(0, c, (2,))
        else:
            weights(c, range(4))
            part = product(0, c, 0, ZN)
        rs_send[:, cols(c)] = part.astype(jnp.bfloat16)
        rs(c).start()

    def part(c):
        acc[:, cols(c)] = product(1, c, 0, 5)

    def own(c):
        acc[:, cols(c)] = product(1, c, 0, ZN)

    def leave(c):
        at = pl.ds(*CHUNKS[c])
        return pltpu.make_async_copy(result.at[:, at], out.at[:, at], out_s.at[c])

    def final(c):
        total = acc[:, cols(c)]
        if c < NC - 2:
            total += product(1, c, 5, ZN)
        rs(c).wait_recv()
        result[:, cols(c)] = (total + rs_recv[:, cols(c)].astype(jnp.float32)).astype(jnp.bfloat16)
        leave(c).start()

    def enter(p):
        v0_arrive(p)
        z_first(0, p)

    def v1_first(p):
        v1_arrive(p)
        z_first(1, p)

    def tile_near():
        tile_x(0, arriving=True).wait_recv()
        tile_x(2).start()

    def statistics():
        tile_x(1, arriving=True).wait_recv()
        tile_x(2, arriving=True).wait_recv()
        means = []
        for lo in (1 - x_lo, x_lo):
            sums = jnp.zeros((8, SUB), jnp.float32)
            for hi in range(2):
                for zz in range(ZN):
                    sums += tiles[2 * hi + lo, zz]
            mean = sums[0:1] / D
            var = sums[1:2] / D - mean * mean
            means += [mean, lax.rsqrt(var + 1e-05)]
        stat[...] = jnp.concatenate(means + [jnp.zeros((124, SUB), jnp.float32)], axis=0).T

    def z_left(v):
        for dirn in range(2):
            for s in range(4):
                for p in range(PIECES[v]):
                    if s < 3 or p in last_hop(dirn, v):
                        z_copy(dirn, v, s, p).wait_send()

    def y_left(c):
        for dirn in range(2):
            for k in range(3):
                y_copy(dirn, c, k).wait_send()

    def drain(stage):
        if stage == 1:
            z_left(1)
            y_left(1)
            for c, i in ((0, 1), (0, 2), (0, 3), (1, 1), (1, 2), (1, 3)):
                d_copy(c, i).wait_send()
            rs(0).wait_send()
            return
        z_left(0)
        y_left(0)
        for c in range(NC):
            d_copy(c, 0).wait_send()
        for k in range(1, ZN):
            tile_z(k).wait_send()
        for k in range(3):
            tile_x(k).wait_send()
        for dirn in range(2):
            for s in range(4):
                for q in range(2):
                    if s < 3 or q == dirn:
                        early_z(dirn, s, q).wait_send()
        for i in range(ZN):
            early_over(i).wait_send()
            early_near(i).wait_send()

        @pl.when(edge)
        def _():
            for p in range(PIECES[1]):
                to_over(p, True).wait_send()
                to_near(p, True).wait_send()

        @pl.when(jnp.logical_not(edge))
        def _():
            for p in range(PIECES[0]):
                to_over(p, False).wait_send()
                to_near(p, False).wait_send()

    tiles_in()
    enter(0)
    relay_on(0)
    early_tick(0)
    enter(1)
    relay_on(1)
    tile_near()
    z_move(0, 0, 0)
    y_tick(0, 0, [(1, 1)])
    early_on(0)
    early_tick(1)
    early_on(1)
    z_move(0, 0, 1)
    early_on(2)
    z_move(0, 1, 0)
    y_tick(0, 1, [(2, 0)])
    statistics()
    z_norm(0, 0, 0)
    z_norm(0, 0, 1)
    early_tick(2)
    z_norm(0, 1, 0)
    normalize_piece(0, 0, 0)
    normalize_piece(0, 1, 0)
    early_on(3)
    y_tick(1, 0, [(2, 1)])
    normalize_early(0)
    z_move(0, 1, 1)
    z_norm(0, 1, 1)
    normalize_early(1)
    normalize_early(2)
    early_on(4)
    z_move(0, 2, 0)
    v1_first(0)
    y_tick(1, 1)
    z_norm(0, 2, 0)
    early_tick(3)
    early_on(5)
    normalize_early(3)
    normalize_piece(1, 0, 0)
    z_move(0, 2, 1)
    v1_first(1)
    z_norm(0, 2, 1)
    normalize_early(4)
    early_on(6)
    normalize_piece(1, 1, 0)
    normalize_early(5)
    early_on(7)
    y_tick(0, 2)
    z_move(0, 3, 0)
    z_move(1, 0, 0)
    z_norm(0, 3, 0)
    normalize_early(6)
    z_norm(1, 0, 0)
    z_move(1, 0, 1)
    z_norm(1, 0, 1)
    y_tick(2, 0, [(3, 0), (3, 1)])
    normalize_early(7)
    give(0)
    z_move(1, 1, 0)
    drain(0)
    z_move(1, 1, 1)
    y_tick(2, 1)
    z_norm(1, 1, 0)
    z_norm(1, 1, 1)
    part(0)
    z_move(1, 2, 0)
    y_tick(1, 2)
    z_norm(1, 2, 0)
    z_move(1, 2, 1)
    y_tick(3, 0)
    give(1)
    part(1)
    z_norm(1, 2, 1)
    z_move(1, 3, 0)
    y_tick(2, 2)
    drain(1)
    y_tick(3, 1)
    give(2)
    y_tick(3, 2)
    z_norm(1, 3, 0)
    own(2)
    before(3)
    give(3)
    own(3)
    final(0)
    final(1)
    final(2)
    final(3)

    for c in range(2, NC):
        y_left(c)
        for i in range(1, 4):
            d_copy(c, i).wait_send()
    for c in range(1, NC):
        rs(c).wait_send()
    for c in range(NC):
        leave(c).wait()


def on_device(tokens, ln_gain, ln_bias, weight):
    vmem = pl.BlockSpec(memory_space=pltpu.VMEM)
    hbm = pl.BlockSpec(memory_space=pl.ANY)
    dma = pltpu.SemaphoreType.DMA
    return pl.pallas_call(
        kernel,
        out_shape=jax.ShapeDtypeStruct((TOK, COLS), jnp.bfloat16),
        in_specs=[hbm, vmem, vmem, hbm],
        out_specs=hbm,
        scratch_shapes=[
            pltpu.VMEM((ZN, 2, TOK, FEAT), jnp.bfloat16),
            pltpu.VMEM((TOK, FEAT), jnp.bfloat16),
            pltpu.VMEM((3, ZN, EARLY, FEAT), jnp.bfloat16),
            pltpu.VMEM((2, TOK, ZN * FEAT), jnp.bfloat16),
            *[pltpu.VMEM((ZN * FEAT, size), jnp.bfloat16) for _, size in CHUNKS],
            pltpu.VMEM((XN, ZN, 8, SUB), jnp.float32),
            pltpu.VMEM((TOK, 128), jnp.float32),
            pltpu.VMEM((TOK, COLS), jnp.float32),
            pltpu.VMEM((TOK, CHUNKS[NC - 1][1]), jnp.float32),
            pltpu.VMEM((TOK, COLS), jnp.bfloat16),
            pltpu.VMEM((TOK, FEAT), jnp.bfloat16),
            pltpu.VMEM((TOK, COLS), jnp.bfloat16),
            pltpu.VMEM((TOK, COLS), jnp.bfloat16),
            dma((4,)), dma((4,)), dma((4,)), dma((2,)), dma((2,)),
            dma((2, 24)), dma((2, 24)),
            dma((2, 3 * NC)), dma((2, 3 * NC)),
            dma((4 * NC,)), dma((4 * NC,)),
            dma((NC,)),
            dma((ZN,)), dma((ZN,)), dma((3,)), dma((3,)),
            dma((NC,)), dma((NC,)),
            dma((2, 8)), dma((2, 8)), dma((ZN,)), dma((ZN,)), dma((ZN,)), dma((ZN,)),
            dma((NC,)), dma(()),
        ],
        compiler_params=pltpu.CompilerParams(collective_id=0, has_side_effects=True, vmem_limit_bytes=58 * 1024 * 1024),
        cost_estimate=pl.CostEstimate(flops=2 * TOK * D * COLS, bytes_accessed=4 * 1024 * 1024, transcendentals=0),
    )(tokens, ln_gain, ln_bias, weight)


def solution(mesh):
    in_specs = (P("row", "col"), P("col"), P("col"), P("row", "col"))
    return jax.shard_map(on_device, mesh=mesh, in_specs=in_specs, out_specs=P("row", "col"), check_vma=False)
```

```python
import jax
import jax.numpy as jnp
from jax import lax
from jax.experimental import pallas as pl
from jax.experimental.pallas import tpu as pltpu
from jax.sharding import PartitionSpec as P

MESH = pl.DeviceIdType.MESH
D = 12288
TOK, FEAT, COLS = 256, 768, 1152
EARLY = 96
PIECES = (2, 2)
HALF = FEAT // 2
CHUNKS = ((0, 512), (512, 256), (768, 256), (1024, 128))
NC = len(CHUNKS)
YN, ZN, XN = 4, 8, 4
SUB = 256


def kernel(tok_in, gain, bias, w, out, xs, relay, zb, nm, wb0, wb1, wb2, wb3, tiles, stat, acc, ahead, result, tok, rs_send, rs_recv,
           bx_s, ax_s, v0_r, v1_r, rl_r, zs_s, zs_r, ys_s, ys_r, dd_s, dd_r, lw_s, tz_s, tz_r, tx_s, tx_r, rs_s, rs_r,
           er_s, er_r, eo_s, eo_r, en_s, en_r, out_s, tok_s, z_ready):
    wb = (wb0, wb1, wb2, wb3)
    row, col = lax.axis_index("row"), lax.axis_index("col")
    core, y, x_lo = row % 2, (row // 2) % YN, row // 8
    z, x_hi = col % ZN, col // ZN
    x = 2 * x_hi + x_lo

    def at(x_hi=x_hi, x_lo=x_lo, y=y, z=z, core=core):
        return ((x_lo * YN + y) * 2 + core, x_hi * ZN + z)

    up, down = at(z=(z + 1) % ZN), at(z=(z + ZN - 1) % ZN)
    fore, back = at(y=(y + 1) % YN), at(y=(y + YN - 1) % YN)
    near = at(x_lo=1 - x_lo)
    over = at(x_hi=1 - x_hi, x_lo=1 - x_lo)
    twin = at(core=1 - core)
    edge = x_lo == x_hi
    edge_index = (x_lo + x_hi + 1) % 2

    def send(src, dst, ssem, rsem, where):
        return pltpu.make_async_remote_copy(src_ref=src, dst_ref=dst, send_sem=ssem, recv_sem=rsem, device_id=where,
                                            device_id_type=MESH)

    def slot(y, core):
        rel = (2 * y + core + ZN - z) % ZN
        return 2 * rel + (rel // 4) * (15 - 4 * rel)

    def block_rows(y, core, start=0, size=FEAT):
        return pl.ds(pl.multiple_of(slot(y, core) * FEAT + start, 128), size)

    tokens_in = pltpu.make_async_copy(tok_in, tok, tok_s)
    tokens_in.start()

    def signal(semaphore, where):
        pl.semaphore_signal(semaphore, inc=1, device_id=where, device_id_type=MESH)

    barrier = pltpu.get_barrier_semaphore()
    even, odd = z % 2 == 0, z % 2 == 1
    for where in (fore, back, near, over, twin):
        signal(barrier, where)

    def own_w(c):
        start, size = CHUNKS[c]
        return pltpu.make_async_copy(w.at[:, pl.ds(start, size)], wb[c].at[block_rows(y, core)], lw_s.at[c])

    for c in range(NC):
        own_w(c).start()
    @pl.when(even)
    def _():
        pl.semaphore_wait(barrier, 5)
        signal(barrier, up)
        signal(barrier, down)

    @pl.when(odd)
    def _():
        pl.semaphore_wait(barrier, 7)
        signal(z_ready.at[0], up)
        signal(z_ready.at[0], down)

    def y_copy(dirn, c, k, arriving=False):
        hops = (1 if arriving else 0) + (1 if k == 2 else 0)
        owner = (y + YN - hops) % YN if dirn == 0 else (y + hops) % YN
        half = ((0, 1, 0)[k] if dirn == 0 else (1, 0, 1)[k]) * HALF
        dst = wb[c].at[block_rows(owner, core, half, HALF)]
        src = dst
        if k < 2 and not arriving:
            start, size = CHUNKS[c]
            src = w.at[pl.ds(half, HALF), pl.ds(start, size)]
        return send(src, dst, ys_s.at[dirn, c * 3 + k], ys_r.at[dirn, c * 3 + k], fore if dirn == 0 else back)

    def d_copy(c, i, arriving=False):
        owner = (y, (y + YN - 1) % YN, (y + 1) % YN, (y + 2) % YN)[i]
        dst = wb[c].at[block_rows(owner, (1 - core) if arriving else core)]
        src = dst
        if i == 0 and not arriving:
            start, size = CHUNKS[c]
            src = w.at[:, pl.ds(start, size)]
        return send(src, dst, dd_s.at[c * 4 + i], dd_r.at[c * 4 + i], twin)

    def rows_of(v, p):
        size = (TOK - EARLY) // PIECES[v]
        return pl.ds(EARLY + p * size, size)

    def z_copy(dirn, v, s, p, arriving=False):
        hops = s + (1 if arriving else 0)
        block = (z + ZN - hops) % ZN if dirn == 0 else (z + hops) % ZN
        ref = xs.at[block, v, rows_of(v, p)]
        k = v * 16 + s * PIECES[v] + p
        return send(ref, ref, zs_s.at[dirn, k], zs_r.at[dirn, k], up if dirn == 0 else down)

    def block_at(i):
        if i == 0:
            return z
        return (z + ZN - (i + 1) // 2) % ZN if i % 2 else (z + i // 2) % ZN

    def early_z(dirn, s, q, arriving=False):
        hops = s + (1 if arriving else 0)
        block = (z + ZN - hops) % ZN if dirn == 0 else (z + hops) % ZN
        ref = zb.at[0, block, pl.ds(q * (EARLY // 2), EARLY // 2)]
        return send(ref, ref, er_s.at[dirn, 2 * s + q], er_r.at[dirn, 2 * s + q], up if dirn == 0 else down)

    def early_over(i):
        block = block_at(i)
        return send(zb.at[0, block], zb.at[1, block], eo_s.at[i], eo_r.at[i], over)

    def early_near(i):
        block = block_at(i)
        return send(zb.at[edge_index, block], zb.at[2, block], en_s.at[i], en_r.at[i], near)

    def early_tick(s):
        for dirn in range(2):
            for q in range(2):
                if s < 3 or q == dirn:
                    early_z(dirn, s, q, arriving=True).wait_recv()
                    if s < 2 or (s == 2 and q == dirn):
                        early_z(dirn, s + 1, q).start()
        for i in (7,) if s == 3 else (2 * s + 1, 2 * s + 2):
            early_over(i).start()

    def early_on(i):
        early_over(i).wait_recv()
        early_near(i).start()

    def to_over(p, edge_case):
        rows = rows_of(1 if edge_case else 0, p)
        dst = relay.at[rows] if edge_case else xs.at[z, 0, rows]
        return send(tok.at[rows], dst, bx_s.at[p], (rl_r if edge_case else v0_r).at[p], over)

    def to_near(p, edge_case):
        rows = rows_of(1 if edge_case else 0, p)
        src = relay.at[rows] if edge_case else tok.at[rows]
        dst = xs.at[z, 1 if edge_case else 0, rows]
        return send(src, dst, ax_s.at[p], (v1_r if edge_case else v0_r).at[p], near)

    def keep(p):
        rows = rows_of(1, p)
        return pltpu.make_async_copy(tok.at[rows], xs.at[z, 1, rows], v1_r.at[p])

    def tile_z(k, arriving=False):
        ref = tiles.at[x, (z + ZN - k) % ZN if arriving else z]
        return send(ref, ref, tz_s.at[k], tz_r.at[k], at(z=(z + k) % ZN))

    def tiles_in():
        for k in range(1, ZN):
            tile_z(k, arriving=True).wait_recv()
        for k in range(2):
            tile_x(k).start()
        early_over(0).start()

    def y_own(c, k):
        for dirn in range(2):
            y_copy(dirn, c, k).start()

    y_own(0, 0)
    y_own(0, 1)
    y_own(1, 0)
    for c in range(NC):
        d_copy(c, 0).start()
    tokens_in.wait()

    @pl.when(edge)
    def _():
        for p in range(PIECES[1]):
            to_over(p, True).start()
            keep(p).start()

    @pl.when(jnp.logical_not(edge))
    def _():
        for p in range(PIECES[0]):
            to_over(p, False).start()
            to_near(p, False).start()

    zb[0, z] = tok[:EARLY]

    @pl.when(even)
    def _():
        pl.semaphore_wait(z_ready.at[0], 2)

    def greet(k):
        signal(z_ready.at[k], up)
        signal(z_ready.at[k], down)

    greet(1)
    for q in range(2):
        for dirn in range(2):
            early_z(dirn, 0, q).start()

    ones = jnp.ones((8, FEAT), jnp.bfloat16)
    over_lanes = (((1,), (1,)), ((), ()))
    values = tok[...]
    wide = values.astype(jnp.float32)
    square = wide * wide
    high = square.astype(jnp.bfloat16)
    low = (square - high.astype(jnp.float32)).astype(jnp.bfloat16)
    total = lax.dot_general(ones, values, over_lanes, preferred_element_type=jnp.float32)
    squares = lax.dot_general(ones, high, over_lanes, preferred_element_type=jnp.float32)
    squares += lax.dot_general(ones, low, over_lanes, preferred_element_type=jnp.float32)
    tiles[x, z, 0:1] = total[0:1]
    tiles[x, z, 1:2] = squares[0:1]
    for j in range(3):
        tiles[x, z, 2 + j:3 + j] = gain[j * SUB:(j + 1) * SUB].astype(jnp.float32).reshape(1, SUB)
        tiles[x, z, 5 + j:6 + j] = bias[j * SUB:(j + 1) * SUB].astype(jnp.float32).reshape(1, SUB)
    for k in range(1, 4):
        pl.semaphore_wait(z_ready.at[k], 2)
        if k < 3:
            greet(k + 1)
    for k in range(1, ZN):
        tile_z(k).start()

    x_near, x_over, x_far = 2 * x_hi + 1 - x_lo, 2 * (1 - x_hi) + 1 - x_lo, 2 * (1 - x_hi) + x_lo

    def tile_x(k, arriving=False):
        ref = tiles.at[(x_near, x_over, x_far)[k] if arriving else (x, x, x_near)[k]]
        return send(ref, ref, tx_s.at[k], tx_r.at[k], near if k == 0 else over)

    def z_first(v, p):
        for dirn in range(2):
            z_copy(dirn, v, 0, p).start()

    def v0_arrive(p):
        to_near(p, False).wait_recv()

    def v1_arrive(p):
        to_near(p, True).wait_recv()

    def relay_on(p):
        @pl.when(edge)
        def _():
            to_over(p, True).wait_recv()
            to_near(p, True).start()

    def y_tick(c, k, own=()):
        for dirn in range(2):
            y_copy(dirn, c, k, arriving=True).wait_recv()
        for piece in own[:1]:
            y_own(*piece)
        if k == 0:
            y_own(c, 2)
        for piece in own[1:]:
            y_own(*piece)
        if k == 1:
            d_copy(c, 1).start()
            d_copy(c, 2).start()
        if k == 2:
            d_copy(c, 3).start()

    def normalize(v, rows, at, block, source):
        mean, scale = stat[rows, 2 * v:2 * v + 1], stat[rows, 2 * v + 1:2 * v + 2]
        for j in range(3):
            lanes = slice(j * SUB, (j + 1) * SUB)
            g = tiles[2 * x_lo, block, 2 + j:3 + j]
            b = tiles[2 * x_lo, block, 5 + j:6 + j]
            part = source[:, lanes].astype(jnp.float32)
            nm[v, rows, at * FEAT + j * SUB:at * FEAT + (j + 1) * SUB] = ((part - mean) * scale * g + b).astype(jnp.bfloat16)

    def normalize_piece(v, p, i):
        size = (TOK - EARLY) // PIECES[v]
        start = EARLY + p * size
        block = block_at(i)
        normalize(v, slice(start, start + size), i, block, xs.at[block, v, pl.ds(start, size)])

    def normalize_early(i):
        block = block_at(i)
        early_near(i).wait_recv()
        normalize(0, slice(0, EARLY), i, block, zb.at[1 + edge_index, block])
        normalize(1, slice(0, EARLY), i, block, zb.at[2 - 2 * edge_index, block])

    def last_hop(dirn, v):
        half = PIECES[v] // 2
        return range(half) if dirn == 0 else range(half, 2 * half)

    def z_move(v, s, p):
        for dirn in range(2):
            piece = last_hop(dirn, v)[p] if s == 3 else p
            z_copy(dirn, v, s, piece, arriving=True).wait_recv()
            if s < 2 or (s == 2 and piece in last_hop(dirn, v)):
                z_copy(dirn, v, s + 1, piece).start()

    def z_norm(v, s, p):
        for dirn in range(2):
            normalize_piece(v, last_hop(dirn, v)[p] if s == 3 else p, 7 if s == 3 else 2 * s + 1 + dirn)

    def product(v, c, first, last):
        k = slice(first * FEAT, last * FEAT)
        return jnp.dot(nm[v, :, k], wb[c][k], preferred_element_type=jnp.float32)

    def product_of(v, c, owners):
        total = None
        for owner in owners:
            for k in range(2):
                at = block_rows((y + owner) % YN, k)
                part = jnp.dot(nm[v, :, at], wb[c][at], preferred_element_type=jnp.float32)
                total = part if total is None else total + part
        return total

    def cols(c):
        start, size = CHUNKS[c]
        return slice(start, start + size)

    def rs(c):
        at = pl.ds(*CHUNKS[c])
        return send(rs_send.at[:, at], rs_recv.at[:, at], rs_s.at[c], rs_r.at[c], near)

    def weights(c, blocks):
        if 0 in blocks:
            own_w(c).wait()
        for i in blocks:
            d_copy(c, i, arriving=True).wait_recv()

    def before(c):
        weights(c, range(3))
        ahead[...] = product_of(0, c, (0, 3, 1))

    def give(c):
        if c == NC - 1:
            weights(c, (3,))
            part = ahead[...] + product_of(0, c, (2,))
        else:
            weights(c, range(4))
            part = product(0, c, 0, ZN)
        rs_send[:, cols(c)] = part.astype(jnp.bfloat16)
        rs(c).start()

    def own(c):
        acc[:, cols(c)] = product(1, c, 0, 7)

    def leave(c):
        at = pl.ds(*CHUNKS[c])
        return pltpu.make_async_copy(result.at[:, at], out.at[:, at], out_s.at[c])

    def final(c):
        total = acc[:, cols(c)] + product(1, c, 7, ZN)
        rs(c).wait_recv()
        result[:, cols(c)] = (total + rs_recv[:, cols(c)].astype(jnp.float32)).astype(jnp.bfloat16)
        leave(c).start()

    def enter(p):
        v0_arrive(p)
        z_first(0, p)

    def v1_first(p):
        v1_arrive(p)
        z_first(1, p)

    def tile_near():
        tile_x(0, arriving=True).wait_recv()
        tile_x(2).start()

    def statistics():
        tile_x(1, arriving=True).wait_recv()
        tile_x(2, arriving=True).wait_recv()
        means = []
        for lo in (1 - x_lo, x_lo):
            sums = jnp.zeros((8, SUB), jnp.float32)
            for hi in range(2):
                for zz in range(ZN):
                    sums += tiles[2 * hi + lo, zz]
            mean = sums[0:1] / D
            var = sums[1:2] / D - mean * mean
            means += [mean, lax.rsqrt(var + 1e-05)]
        stat[...] = jnp.concatenate(means + [jnp.zeros((124, SUB), jnp.float32)], axis=0).T

    def z_left(v):
        for dirn in range(2):
            for s in range(4):
                for p in range(PIECES[v]):
                    if s < 3 or p in last_hop(dirn, v):
                        z_copy(dirn, v, s, p).wait_send()

    def y_left(c):
        for dirn in range(2):
            for k in range(3):
                y_copy(dirn, c, k).wait_send()

    def drain(stage):
        if stage == 1:
            z_left(1)
            y_left(1)
            for c, i in ((0, 1), (0, 2), (0, 3), (1, 1), (1, 2), (1, 3)):
                d_copy(c, i).wait_send()
            rs(0).wait_send()
            return
        z_left(0)
        y_left(0)
        for c in range(NC):
            d_copy(c, 0).wait_send()
        for k in range(1, ZN):
            tile_z(k).wait_send()
        for k in range(3):
            tile_x(k).wait_send()
        for dirn in range(2):
            for s in range(4):
                for q in range(2):
                    if s < 3 or q == dirn:
                        early_z(dirn, s, q).wait_send()
        for i in range(ZN):
            early_over(i).wait_send()
            early_near(i).wait_send()

        @pl.when(edge)
        def _():
            for p in range(PIECES[1]):
                to_over(p, True).wait_send()
                to_near(p, True).wait_send()

        @pl.when(jnp.logical_not(edge))
        def _():
            for p in range(PIECES[0]):
                to_over(p, False).wait_send()
                to_near(p, False).wait_send()

    enter(0)
    relay_on(0)
    enter(1)
    relay_on(1)
    tiles_in()
    early_tick(0)
    y_tick(0, 0, [(1, 1)])
    z_move(0, 0, 0)
    tile_near()
    z_move(0, 0, 1)
    early_on(0)
    early_tick(1)
    y_tick(0, 1, [(2, 0)])
    early_on(1)
    z_move(0, 1, 0)
    early_on(2)
    y_tick(1, 0, [(2, 1)])
    z_move(0, 1, 1)
    statistics()
    z_norm(0, 0, 0)
    z_norm(0, 0, 1)
    z_norm(0, 1, 0)
    z_norm(0, 1, 1)
    early_tick(2)
    y_tick(1, 1)
    early_on(3)
    normalize_piece(0, 0, 0)
    normalize_piece(0, 1, 0)
    normalize_early(0)
    normalize_early(1)
    z_move(0, 2, 0)
    early_on(4)
    v1_first(0)
    z_norm(0, 2, 0)
    normalize_early(2)
    normalize_piece(1, 0, 0)
    z_move(0, 2, 1)
    v1_first(1)
    z_norm(0, 2, 1)
    early_on(5)
    normalize_early(3)
    early_tick(3)
    normalize_piece(1, 1, 0)
    y_tick(0, 2)
    early_on(6)
    normalize_early(4)
    z_move(0, 3, 0)
    z_move(1, 0, 0)
    early_on(7)
    y_tick(2, 0, [(3, 0), (3, 1)])
    z_norm(0, 3, 0)
    normalize_early(5)
    z_move(1, 0, 1)
    z_norm(1, 0, 0)
    z_norm(1, 0, 1)
    normalize_early(6)
    z_move(1, 1, 0)
    y_tick(2, 1)
    z_norm(1, 1, 0)
    normalize_early(7)
    give(0)
    z_move(1, 1, 1)
    y_tick(1, 2)
    drain(0)
    y_tick(3, 0)
    z_move(1, 2, 0)
    give(1)
    z_move(1, 2, 1)
    z_norm(1, 1, 1)
    z_norm(1, 2, 0)
    z_norm(1, 2, 1)
    y_tick(2, 2)
    own(0)
    y_tick(3, 1)
    z_move(1, 3, 0)
    give(2)
    y_tick(3, 2)
    own(2)
    before(3)
    give(3)
    own(3)
    own(1)
    drain(1)
    z_norm(1, 3, 0)
    final(0)
    final(1)
    final(2)
    final(3)

    for c in range(2, NC):
        y_left(c)
        for i in range(1, 4):
            d_copy(c, i).wait_send()
    for c in range(1, NC):
        rs(c).wait_send()
    for c in range(NC):
        leave(c).wait()


def on_device(tokens, ln_gain, ln_bias, weight):
    vmem = pl.BlockSpec(memory_space=pltpu.VMEM)
    hbm = pl.BlockSpec(memory_space=pl.ANY)
    dma = pltpu.SemaphoreType.DMA
    return pl.pallas_call(
        kernel,
        out_shape=jax.ShapeDtypeStruct((TOK, COLS), jnp.bfloat16),
        in_specs=[hbm, vmem, vmem, hbm],
        out_specs=hbm,
        scratch_shapes=[
            pltpu.VMEM((ZN, 2, TOK, FEAT), jnp.bfloat16),
            pltpu.VMEM((TOK, FEAT), jnp.bfloat16),
            pltpu.VMEM((3, ZN, EARLY, FEAT), jnp.bfloat16),
            pltpu.VMEM((2, TOK, ZN * FEAT), jnp.bfloat16),
            *[pltpu.VMEM((ZN * FEAT, size), jnp.bfloat16) for _, size in CHUNKS],
            pltpu.VMEM((XN, ZN, 8, SUB), jnp.float32),
            pltpu.VMEM((TOK, 128), jnp.float32),
            pltpu.VMEM((TOK, COLS), jnp.float32),
            pltpu.VMEM((TOK, CHUNKS[NC - 1][1]), jnp.float32),
            pltpu.VMEM((TOK, COLS), jnp.bfloat16),
            pltpu.VMEM((TOK, FEAT), jnp.bfloat16),
            pltpu.VMEM((TOK, COLS), jnp.bfloat16),
            pltpu.VMEM((TOK, COLS), jnp.bfloat16),
            dma((4,)), dma((4,)), dma((4,)), dma((2,)), dma((2,)),
            dma((2, 24)), dma((2, 24)),
            dma((2, 3 * NC)), dma((2, 3 * NC)),
            dma((4 * NC,)), dma((4 * NC,)),
            dma((NC,)),
            dma((ZN,)), dma((ZN,)), dma((3,)), dma((3,)),
            dma((NC,)), dma((NC,)),
            dma((2, 8)), dma((2, 8)), dma((ZN,)), dma((ZN,)), dma((ZN,)), dma((ZN,)),
            dma((NC,)), dma(()), pltpu.SemaphoreType.REGULAR((4,)),
        ],
        compiler_params=pltpu.CompilerParams(collective_id=0, has_side_effects=True, vmem_limit_bytes=58 * 1024 * 1024),
        cost_estimate=pl.CostEstimate(flops=2 * TOK * D * COLS, bytes_accessed=4 * 1024 * 1024, transcendentals=0),
    )(tokens, ln_gain, ln_bias, weight)


def solution(mesh):
    in_specs = (P("row", "col"), P("col"), P("col"), P("row", "col"))
    return jax.shard_map(on_device, mesh=mesh, in_specs=in_specs, out_specs=P("row", "col"), check_vma=False)
```

```python
import jax
import jax.numpy as jnp
from jax import lax
from jax.experimental import pallas as pl
from jax.experimental.pallas import tpu as pltpu
from jax.sharding import PartitionSpec as P

MESH = pl.DeviceIdType.MESH
D = 12288
TOK, FEAT, COLS = 256, 768, 1152
EARLY = 96
PIECES = (2, 2)
HALF = FEAT // 2
CHUNKS = ((0, 512), (512, 256), (768, 256), (1024, 128))
NC = len(CHUNKS)
YN, ZN, XN = 4, 8, 4
SUB = 256


def kernel(tok_in, gain, bias, w, out, xs, relay, zb, nm, wb0, wb1, wb2, wb3, tiles, stat, acc, ahead, result, tok, rs_send, rs_recv,
           bx_s, ax_s, v0_r, v1_r, rl_r, zs_s, zs_r, ys_s, ys_r, dd_s, dd_r, lw_s, tz_s, tz_r, tx_s, tx_r, rs_s, rs_r,
           er_s, er_r, eo_s, eo_r, en_s, en_r, out_s, tok_s, z_ready):
    wb = (wb0, wb1, wb2, wb3)
    row, col = lax.axis_index("row"), lax.axis_index("col")
    core, y, x_lo = row % 2, (row // 2) % YN, row // 8
    z, x_hi = col % ZN, col // ZN
    x = 2 * x_hi + x_lo

    def at(x_hi=x_hi, x_lo=x_lo, y=y, z=z, core=core):
        return ((x_lo * YN + y) * 2 + core, x_hi * ZN + z)

    up, down = at(z=(z + 1) % ZN), at(z=(z + ZN - 1) % ZN)
    fore, back = at(y=(y + 1) % YN), at(y=(y + YN - 1) % YN)
    near = at(x_lo=1 - x_lo)
    over = at(x_hi=1 - x_hi, x_lo=1 - x_lo)
    twin = at(core=1 - core)
    edge = x_lo == x_hi
    edge_index = (x_lo + x_hi + 1) % 2

    def send(src, dst, ssem, rsem, where):
        return pltpu.make_async_remote_copy(src_ref=src, dst_ref=dst, send_sem=ssem, recv_sem=rsem, device_id=where,
                                            device_id_type=MESH)

    def slot(y, core):
        rel = (2 * y + core + ZN - z) % ZN
        return 2 * rel + (rel // 4) * (15 - 4 * rel)

    def block_rows(y, core, start=0, size=FEAT):
        return pl.ds(pl.multiple_of(slot(y, core) * FEAT + start, 128), size)

    tokens_in = pltpu.make_async_copy(tok_in, tok, tok_s)
    tokens_in.start()

    def signal(semaphore, where):
        pl.semaphore_signal(semaphore, inc=1, device_id=where, device_id_type=MESH)

    barrier = pltpu.get_barrier_semaphore()
    even, odd = z % 2 == 0, z % 2 == 1
    for where in (fore, back, near, over, twin):
        signal(barrier, where)

    def own_w(c):
        start, size = CHUNKS[c]
        return pltpu.make_async_copy(w.at[:, pl.ds(start, size)], wb[c].at[block_rows(y, core)], lw_s.at[c])

    for c in range(NC):
        own_w(c).start()
    @pl.when(even)
    def _():
        pl.semaphore_wait(barrier, 5)
        signal(barrier, up)
        signal(barrier, down)

    @pl.when(odd)
    def _():
        pl.semaphore_wait(barrier, 7)
        signal(z_ready.at[0], up)
        signal(z_ready.at[0], down)

    def y_copy(dirn, c, k, arriving=False):
        hops = (1 if arriving else 0) + (1 if k == 2 else 0)
        owner = (y + YN - hops) % YN if dirn == 0 else (y + hops) % YN
        half = ((0, 1, 0)[k] if dirn == 0 else (1, 0, 1)[k]) * HALF
        dst = wb[c].at[block_rows(owner, core, half, HALF)]
        src = dst
        if k < 2 and not arriving:
            start, size = CHUNKS[c]
            src = w.at[pl.ds(half, HALF), pl.ds(start, size)]
        return send(src, dst, ys_s.at[dirn, c * 3 + k], ys_r.at[dirn, c * 3 + k], fore if dirn == 0 else back)

    def d_copy(c, i, arriving=False):
        owner = (y, (y + YN - 1) % YN, (y + 1) % YN, (y + 2) % YN)[i]
        dst = wb[c].at[block_rows(owner, (1 - core) if arriving else core)]
        src = dst
        if i == 0 and not arriving:
            start, size = CHUNKS[c]
            src = w.at[:, pl.ds(start, size)]
        return send(src, dst, dd_s.at[c * 4 + i], dd_r.at[c * 4 + i], twin)

    def rows_of(v, p):
        size = (TOK - EARLY) // PIECES[v]
        return pl.ds(EARLY + p * size, size)

    def z_copy(dirn, v, s, p, arriving=False):
        hops = s + (1 if arriving else 0)
        block = (z + ZN - hops) % ZN if dirn == 0 else (z + hops) % ZN
        ref = xs.at[block, v, rows_of(v, p)]
        k = v * 16 + s * PIECES[v] + p
        return send(ref, ref, zs_s.at[dirn, k], zs_r.at[dirn, k], up if dirn == 0 else down)

    def block_at(i):
        if i == 0:
            return z
        return (z + ZN - (i + 1) // 2) % ZN if i % 2 else (z + i // 2) % ZN

    def early_z(dirn, s, q, arriving=False):
        hops = s + (1 if arriving else 0)
        block = (z + ZN - hops) % ZN if dirn == 0 else (z + hops) % ZN
        ref = zb.at[0, block, pl.ds(q * (EARLY // 2), EARLY // 2)]
        return send(ref, ref, er_s.at[dirn, 2 * s + q], er_r.at[dirn, 2 * s + q], up if dirn == 0 else down)

    def early_over(i):
        block = block_at(i)
        return send(zb.at[0, block], zb.at[1, block], eo_s.at[i], eo_r.at[i], over)

    def early_near(i):
        block = block_at(i)
        return send(zb.at[edge_index, block], zb.at[2, block], en_s.at[i], en_r.at[i], near)

    def early_tick(s):
        for dirn in range(2):
            for q in range(2):
                if s < 3 or q == dirn:
                    early_z(dirn, s, q, arriving=True).wait_recv()
                    if s < 2 or (s == 2 and q == dirn):
                        early_z(dirn, s + 1, q).start()
        for i in (7,) if s == 3 else (2 * s + 1, 2 * s + 2):
            early_over(i).start()

    def early_on(i):
        early_over(i).wait_recv()
        early_near(i).start()

    def to_over(p, edge_case):
        rows = rows_of(1 if edge_case else 0, p)
        dst = relay.at[rows] if edge_case else xs.at[z, 0, rows]
        return send(tok.at[rows], dst, bx_s.at[p], (rl_r if edge_case else v0_r).at[p], over)

    def to_near(p, edge_case):
        rows = rows_of(1 if edge_case else 0, p)
        src = relay.at[rows] if edge_case else tok.at[rows]
        dst = xs.at[z, 1 if edge_case else 0, rows]
        return send(src, dst, ax_s.at[p], (v1_r if edge_case else v0_r).at[p], near)

    def keep(p):
        rows = rows_of(1, p)
        return pltpu.make_async_copy(tok.at[rows], xs.at[z, 1, rows], v1_r.at[p])

    def tile_z(k, arriving=False):
        ref = tiles.at[x, (z + ZN - k) % ZN if arriving else z]
        return send(ref, ref, tz_s.at[k], tz_r.at[k], at(z=(z + k) % ZN))

    def tiles_in():
        for k in range(1, ZN):
            tile_z(k, arriving=True).wait_recv()
        for k in range(2):
            tile_x(k).start()
        early_over(0).start()

    def y_own(c, k):
        for dirn in range(2):
            y_copy(dirn, c, k).start()

    y_own(0, 0)
    y_own(0, 1)
    y_own(1, 0)
    for c in range(NC):
        d_copy(c, 0).start()
    tokens_in.wait()

    @pl.when(edge)
    def _():
        for p in range(PIECES[1]):
            to_over(p, True).start()
            keep(p).start()

    @pl.when(jnp.logical_not(edge))
    def _():
        for p in range(PIECES[0]):
            to_over(p, False).start()
            to_near(p, False).start()

    zb[0, z] = tok[:EARLY]

    @pl.when(even)
    def _():
        pl.semaphore_wait(z_ready.at[0], 2)

    def greet(k):
        signal(z_ready.at[k], up)
        signal(z_ready.at[k], down)

    greet(1)
    for q in range(2):
        for dirn in range(2):
            early_z(dirn, 0, q).start()

    ones = jnp.ones((8, FEAT), jnp.bfloat16)
    over_lanes = (((1,), (1,)), ((), ()))
    values = tok[...]
    wide = values.astype(jnp.float32)
    square = wide * wide
    high = square.astype(jnp.bfloat16)
    low = (square - high.astype(jnp.float32)).astype(jnp.bfloat16)
    total = lax.dot_general(ones, values, over_lanes, preferred_element_type=jnp.float32)
    squares = lax.dot_general(ones, high, over_lanes, preferred_element_type=jnp.float32)
    squares += lax.dot_general(ones, low, over_lanes, preferred_element_type=jnp.float32)
    tiles[x, z, 0:1] = total[0:1]
    tiles[x, z, 1:2] = squares[0:1]
    for j in range(3):
        tiles[x, z, 2 + j:3 + j] = gain[j * SUB:(j + 1) * SUB].astype(jnp.float32).reshape(1, SUB)
        tiles[x, z, 5 + j:6 + j] = bias[j * SUB:(j + 1) * SUB].astype(jnp.float32).reshape(1, SUB)
    for k in range(1, 4):
        pl.semaphore_wait(z_ready.at[k], 2)
        if k < 3:
            greet(k + 1)
    for k in range(1, ZN):
        tile_z(k).start()

    x_near, x_over, x_far = 2 * x_hi + 1 - x_lo, 2 * (1 - x_hi) + 1 - x_lo, 2 * (1 - x_hi) + x_lo

    def tile_x(k, arriving=False):
        ref = tiles.at[(x_near, x_over, x_far)[k] if arriving else (x, x, x_near)[k]]
        return send(ref, ref, tx_s.at[k], tx_r.at[k], near if k == 0 else over)

    def z_first(v, p):
        for dirn in range(2):
            z_copy(dirn, v, 0, p).start()

    def v0_arrive(p):
        to_near(p, False).wait_recv()

    def v1_arrive(p):
        to_near(p, True).wait_recv()

    def relay_on(p):
        @pl.when(edge)
        def _():
            to_over(p, True).wait_recv()
            to_near(p, True).start()

    def y_tick(c, k, own=()):
        for dirn in range(2):
            y_copy(dirn, c, k, arriving=True).wait_recv()
        for piece in own[:1]:
            y_own(*piece)
        if k == 0:
            y_own(c, 2)
        for piece in own[1:]:
            y_own(*piece)
        if k == 1:
            d_copy(c, 1).start()
            d_copy(c, 2).start()
        if k == 2:
            d_copy(c, 3).start()

    def normalize(v, rows, at, block, source):
        mean, scale = stat[rows, 2 * v:2 * v + 1], stat[rows, 2 * v + 1:2 * v + 2]
        for j in range(3):
            lanes = slice(j * SUB, (j + 1) * SUB)
            g = tiles[2 * x_lo, block, 2 + j:3 + j]
            b = tiles[2 * x_lo, block, 5 + j:6 + j]
            part = source[:, lanes].astype(jnp.float32)
            nm[v, rows, at * FEAT + j * SUB:at * FEAT + (j + 1) * SUB] = ((part - mean) * scale * g + b).astype(jnp.bfloat16)

    def normalize_piece(v, p, i):
        size = (TOK - EARLY) // PIECES[v]
        start = EARLY + p * size
        block = block_at(i)
        normalize(v, slice(start, start + size), i, block, xs.at[block, v, pl.ds(start, size)])

    def normalize_early(i):
        block = block_at(i)
        early_near(i).wait_recv()
        normalize(0, slice(0, EARLY), i, block, zb.at[1 + edge_index, block])
        normalize(1, slice(0, EARLY), i, block, zb.at[2 - 2 * edge_index, block])

    def last_hop(dirn, v):
        half = PIECES[v] // 2
        return range(half) if dirn == 0 else range(half, 2 * half)

    def z_move(v, s, p):
        for dirn in range(2):
            piece = last_hop(dirn, v)[p] if s == 3 else p
            z_copy(dirn, v, s, piece, arriving=True).wait_recv()
            if s < 2 or (s == 2 and piece in last_hop(dirn, v)):
                z_copy(dirn, v, s + 1, piece).start()

    def z_norm(v, s, p):
        for dirn in range(2):
            normalize_piece(v, last_hop(dirn, v)[p] if s == 3 else p, 7 if s == 3 else 2 * s + 1 + dirn)

    def product(v, c, first, last):
        k = slice(first * FEAT, last * FEAT)
        return jnp.dot(nm[v, :, k], wb[c][k], preferred_element_type=jnp.float32)

    def product_of(v, c, owners):
        total = None
        for owner in owners:
            for k in range(2):
                at = block_rows((y + owner) % YN, k)
                part = jnp.dot(nm[v, :, at], wb[c][at], preferred_element_type=jnp.float32)
                total = part if total is None else total + part
        return total

    def cols(c):
        start, size = CHUNKS[c]
        return slice(start, start + size)

    def rs(c):
        at = pl.ds(*CHUNKS[c])
        return send(rs_send.at[:, at], rs_recv.at[:, at], rs_s.at[c], rs_r.at[c], near)

    def weights(c, blocks):
        if 0 in blocks:
            own_w(c).wait()
        for i in blocks:
            d_copy(c, i, arriving=True).wait_recv()

    def before(c):
        weights(c, range(3))
        ahead[...] = product_of(0, c, (0, 3, 1))

    def give(c):
        if c == NC - 1:
            weights(c, (3,))
            part = ahead[...] + product_of(0, c, (2,))
        else:
            weights(c, range(4))
            part = product(0, c, 0, ZN)
        rs_send[:, cols(c)] = part.astype(jnp.bfloat16)
        rs(c).start()

    def own(c):
        acc[:, cols(c)] = product(1, c, 0, 7)

    def leave(c):
        at = pl.ds(*CHUNKS[c])
        return pltpu.make_async_copy(result.at[:, at], out.at[:, at], out_s.at[c])

    def final(c):
        total = acc[:, cols(c)] + product(1, c, 7, ZN)
        rs(c).wait_recv()
        result[:, cols(c)] = (total + rs_recv[:, cols(c)].astype(jnp.float32)).astype(jnp.bfloat16)
        leave(c).start()

    def enter(p):
        v0_arrive(p)
        z_first(0, p)

    def v1_first(p):
        v1_arrive(p)
        z_first(1, p)

    def tile_near():
        tile_x(0, arriving=True).wait_recv()
        tile_x(2).start()

    def statistics():
        tile_x(1, arriving=True).wait_recv()
        tile_x(2, arriving=True).wait_recv()
        means = []
        for lo in (1 - x_lo, x_lo):
            sums = jnp.zeros((8, SUB), jnp.float32)
            for hi in range(2):
                for zz in range(ZN):
                    sums += tiles[2 * hi + lo, zz]
            mean = sums[0:1] / D
            var = sums[1:2] / D - mean * mean
            means += [mean, lax.rsqrt(var + 1e-05)]
        stat[...] = jnp.concatenate(means + [jnp.zeros((124, SUB), jnp.float32)], axis=0).T

    def z_left(v):
        for dirn in range(2):
            for s in range(4):
                for p in range(PIECES[v]):
                    if s < 3 or p in last_hop(dirn, v):
                        z_copy(dirn, v, s, p).wait_send()

    def y_left(c):
        for dirn in range(2):
            for k in range(3):
                y_copy(dirn, c, k).wait_send()

    def drain(stage):
        if stage == 1:
            z_left(1)
            y_left(1)
            for c, i in ((0, 1), (0, 2), (0, 3), (1, 1), (1, 2), (1, 3)):
                d_copy(c, i).wait_send()
            rs(0).wait_send()
            return
        z_left(0)
        y_left(0)
        for c in range(NC):
            d_copy(c, 0).wait_send()
        for k in range(1, ZN):
            tile_z(k).wait_send()
        for k in range(3):
            tile_x(k).wait_send()
        for dirn in range(2):
            for s in range(4):
                for q in range(2):
                    if s < 3 or q == dirn:
                        early_z(dirn, s, q).wait_send()
        for i in range(ZN):
            early_over(i).wait_send()
            early_near(i).wait_send()

        @pl.when(edge)
        def _():
            for p in range(PIECES[1]):
                to_over(p, True).wait_send()
                to_near(p, True).wait_send()

        @pl.when(jnp.logical_not(edge))
        def _():
            for p in range(PIECES[0]):
                to_over(p, False).wait_send()
                to_near(p, False).wait_send()

    enter(0)
    relay_on(0)
    enter(1)
    relay_on(1)
    tiles_in()
    early_tick(0)
    y_tick(0, 0, [(1, 1)])
    z_move(0, 0, 0)
    tile_near()
    z_move(0, 0, 1)
    early_on(0)
    early_tick(1)
    y_tick(0, 1, [(2, 0)])
    early_on(1)
    z_move(0, 1, 0)
    early_on(2)
    y_tick(1, 0, [(2, 1)])
    z_move(0, 1, 1)
    statistics()
    z_norm(0, 0, 0)
    z_norm(0, 0, 1)
    z_norm(0, 1, 0)
    z_norm(0, 1, 1)
    early_tick(2)
    y_tick(1, 1)
    early_on(3)
    normalize_piece(0, 0, 0)
    normalize_piece(0, 1, 0)
    normalize_early(0)
    normalize_early(1)
    z_move(0, 2, 0)
    early_on(4)
    v1_first(0)
    z_norm(0, 2, 0)
    normalize_early(2)
    normalize_piece(1, 0, 0)
    z_move(0, 2, 1)
    v1_first(1)
    z_norm(0, 2, 1)
    early_on(5)
    normalize_early(3)
    early_tick(3)
    normalize_piece(1, 1, 0)
    y_tick(0, 2)
    early_on(6)
    normalize_early(4)
    z_move(0, 3, 0)
    z_move(1, 0, 0)
    early_on(7)
    y_tick(2, 0, [(3, 0), (3, 1)])
    z_norm(0, 3, 0)
    normalize_early(5)
    z_move(1, 0, 1)
    z_norm(1, 0, 0)
    z_norm(1, 0, 1)
    normalize_early(6)
    z_move(1, 1, 0)
    y_tick(2, 1)
    z_norm(1, 1, 0)
    normalize_early(7)
    give(0)
    z_move(1, 1, 1)
    y_tick(1, 2)
    drain(0)
    y_tick(3, 0)
    z_move(1, 2, 0)
    give(1)
    z_move(1, 2, 1)
    z_norm(1, 1, 1)
    z_norm(1, 2, 0)
    z_norm(1, 2, 1)
    y_tick(2, 2)
    own(0)
    own(1)
    y_tick(3, 1)
    give(2)
    y_tick(3, 2)
    own(2)
    before(3)
    give(3)
    own(3)
    z_move(1, 3, 0)
    z_norm(1, 3, 0)
    final(0)
    final(1)
    final(2)
    final(3)
    drain(1)

    for c in range(2, NC):
        y_left(c)
        for i in range(1, 4):
            d_copy(c, i).wait_send()
    for c in range(1, NC):
        rs(c).wait_send()
    for c in range(NC):
        leave(c).wait()


def on_device(tokens, ln_gain, ln_bias, weight):
    vmem = pl.BlockSpec(memory_space=pltpu.VMEM)
    hbm = pl.BlockSpec(memory_space=pl.ANY)
    dma = pltpu.SemaphoreType.DMA
    return pl.pallas_call(
        kernel,
        out_shape=jax.ShapeDtypeStruct((TOK, COLS), jnp.bfloat16),
        in_specs=[hbm, vmem, vmem, hbm],
        out_specs=hbm,
        scratch_shapes=[
            pltpu.VMEM((ZN, 2, TOK, FEAT), jnp.bfloat16),
            pltpu.VMEM((TOK, FEAT), jnp.bfloat16),
            pltpu.VMEM((3, ZN, EARLY, FEAT), jnp.bfloat16),
            pltpu.VMEM((2, TOK, ZN * FEAT), jnp.bfloat16),
            *[pltpu.VMEM((ZN * FEAT, size), jnp.bfloat16) for _, size in CHUNKS],
            pltpu.VMEM((XN, ZN, 8, SUB), jnp.float32),
            pltpu.VMEM((TOK, 128), jnp.float32),
            pltpu.VMEM((TOK, COLS), jnp.float32),
            pltpu.VMEM((TOK, CHUNKS[NC - 1][1]), jnp.float32),
            pltpu.VMEM((TOK, COLS), jnp.bfloat16),
            pltpu.VMEM((TOK, FEAT), jnp.bfloat16),
            pltpu.VMEM((TOK, COLS), jnp.bfloat16),
            pltpu.VMEM((TOK, COLS), jnp.bfloat16),
            dma((4,)), dma((4,)), dma((4,)), dma((2,)), dma((2,)),
            dma((2, 24)), dma((2, 24)),
            dma((2, 3 * NC)), dma((2, 3 * NC)),
            dma((4 * NC,)), dma((4 * NC,)),
            dma((NC,)),
            dma((ZN,)), dma((ZN,)), dma((3,)), dma((3,)),
            dma((NC,)), dma((NC,)),
            dma((2, 8)), dma((2, 8)), dma((ZN,)), dma((ZN,)), dma((ZN,)), dma((ZN,)),
            dma((NC,)), dma(()), pltpu.SemaphoreType.REGULAR((4,)),
        ],
        compiler_params=pltpu.CompilerParams(collective_id=0, has_side_effects=True, vmem_limit_bytes=58 * 1024 * 1024),
        cost_estimate=pl.CostEstimate(flops=2 * TOK * D * COLS, bytes_accessed=4 * 1024 * 1024, transcendentals=0),
    )(tokens, ln_gain, ln_bias, weight)


def solution(mesh):
    in_specs = (P("row", "col"), P("col"), P("col"), P("row", "col"))
    return jax.shard_map(on_device, mesh=mesh, in_specs=in_specs, out_specs=P("row", "col"), check_vma=False)
```
